256 devices in a mesh: rep: 32 (over y, x, core), tp: 8 (over z).
Axes of the slice: x: 4, y: 4, z: 8, core: 2. Of those that a mesh axis runs over, the one named last changes fastest.
Arguments:
- hidden_in: bfloat16 [256, 5120], P('rep'), may hold values from -40 to 40
- key_cache: bfloat16 [256, 8, 256, 128], P('rep', 'tp'), may hold values from -250 to 250
- value_cache: bfloat16 [256, 8, 256, 128], P('rep', 'tp'), may hold values from -6 to 6
- query_weight: bfloat16 [5120, 3072], P(None, 'tp'), may hold values from -0.078125 to 0.078125
- key_weight: bfloat16 [5120, 1024], P(None, 'tp'), may hold values from -0.078125 to 0.078125
- value_weight: bfloat16 [5120, 1024], P(None, 'tp'), may hold values from -0.078125 to 0.078125
- output_weight: bfloat16 [3072, 5120], P('tp'), may hold values from -0.3125 to 0.3125
- norm_gain: bfloat16 [5120], replicated, may hold values from 0.099609375 to 1.8984375
- countdown_table: bfloat16 [32, 5120], replicated, may hold values from -3 to 3
- countdown_ids: int32 [2, 256], P(None, 'rep'), may hold values from 0 to 31
- lengths: int32 [256], replicated, may hold values from 16 to 254, as said below
- source_slot: int32 [2, 256], replicated, may hold values from 0 to 255, as said below
Outputs:
- hidden_out: bfloat16 [2, 256, 5120], P(None, 'rep')
The draws below stay inside these ranges and needn't reach their ends.
Inputs may be any that keep to these rules, and one draw needn't show every extreme that they name: `source_slot`: in each step the slots form a permutation; each replica hands exactly 2 rows to other replicas and takes exactly 2, never two from the same replica, into the slots that its leaving rows freed; all other rows keep their slots. In each step there are 2 distinct offsets d, the same for every replica: replica r hands one row to each replica (r + d) mod 32. One offset is 1 in even steps and 32 // 2 in odd steps; the others are drawn. `lengths`: some row holds exactly 254 tokens, some exactly 16.
All inputs are finite; a program needn't handle non-finite values.
Results may differ from the reference program's by a relative error of at most 0.011.
Values may be sent and summed in bfloat16 or wider, within the bound.
A program may use at most 64 MiB of HBM per device.

```python
import jax
import jax.numpy as jnp
from jax import lax

D = 5120
HD = 128
KVH = 8
GROUP = 3
HQ = 24
R = 8
CACHE = 256
MOVE = 2
STEPS = 2
COUNT_TOKENS = 32
ROWS = 256


def spread_scale(key, count, lowest, highest):
    return jnp.exp(jax.random.uniform(key, (count,), jnp.float32, jnp.log(lowest), jnp.log(highest)))


def draw_hidden_in(key, part):
    key = jax.random.fold_in(key, 41)
    keys_list = jax.random.split(key, 3)
    row_scale = spread_scale(keys_list[0], ROWS, 0.3, 3.0)
    column_scale = spread_scale(keys_list[1], D, 0.3, 3.0)
    noise = jax.random.normal(keys_list[2], (ROWS, D), jnp.float32)
    return jnp.clip(noise * row_scale[:, None] * column_scale[None, :], -40.0, 40.0).astype(jnp.bfloat16)


def draw_key_cache(key, part):
    key = jax.random.fold_in(key, 37)
    keys_list = jax.random.split(key, 2)
    dimensions = (ROWS, KVH, CACHE, HD)
    values_drawn = jax.random.normal(keys_list[1], dimensions, jnp.float32)
    return jnp.clip(values_drawn, -250.0, 250.0).astype(jnp.bfloat16)


def draw_lengths(key, part):
    key = jax.random.fold_in(key, 11)
    keys_list = jax.random.split(key, 3)
    replicas = ROWS // R
    ceiling = jax.random.randint(keys_list[0], (replicas, 1), 24, CACHE - STEPS + 1)
    drawn = jax.random.randint(keys_list[1], (replicas, R), 16, ceiling + 1).reshape(ROWS)
    ordering = jax.random.permutation(keys_list[2], ROWS)
    drawn = drawn.at[ordering[0]].set(CACHE - STEPS).at[ordering[1]].set(16)
    return drawn.astype(jnp.int32)


def draw_source_slot(key, part):
    key = jax.random.fold_in(key, 23)
    replicas = ROWS // R
    everywhere = jnp.arange(ROWS, dtype=jnp.int32)
    receivers = jnp.arange(replicas, dtype=jnp.int32)
    tables = []
    for step_index in range(STEPS):
        keys_list = jax.random.split(jax.random.fold_in(key, step_index), 3)
        orders = jax.vmap(lambda single: jax.random.permutation(single, R))(jax.random.split(keys_list[0], replicas))
        leaving = orders[:, :MOVE].astype(jnp.int32)
        fixed_offset = 1 if step_index % 2 == 0 else replicas // 2
        candidates = jnp.array([value for value in range(1, replicas) if value != fixed_offset], dtype=jnp.int32)
        picked = jax.random.permutation(keys_list[2], replicas - 2)[:MOVE - 1]
        offsets = jnp.concatenate([jnp.array([fixed_offset], dtype=jnp.int32), jnp.take(candidates, picked)]).astype(jnp.int32)
        table = everywhere
        for order_index in range(MOVE):
            senders = (receivers - offsets[order_index]) % replicas
            table = table.at[receivers * R + leaving[receivers, order_index]].set(senders * R + leaving[senders, order_index])
        tables.append(table)
    return jnp.stack(tables).astype(jnp.int32)


def with_ends(values, stream_key, low, high):
    longest = values.shape.index(max(values.shape))
    spots = []
    for shift in (0, 1):
        where = [jax.random.randint(jax.random.fold_in(stream_key, axis), (), 0, length) for axis, length in enumerate(values.shape)]
        where[longest] = (where[longest] + shift) % values.shape[longest]
        spots.append(tuple(where))
    return values.at[spots[0]].set(low).at[spots[1]].set(high)


def block_levels(stream_key, extent, cuts, smallest, top_value):
    level, own = 1.0, jax.random.fold_in(stream_key, 6)
    for axis_at, shards_of in cuts:
        draws = jnp.exp(jax.random.uniform(jax.random.fold_in(own, axis_at), (shards_of,), jnp.float32, smallest / len(cuts), top_value / len(cuts)))
        level = level * jnp.repeat(draws, extent[axis_at] // shards_of).reshape([-1 if axis == axis_at else 1 for axis in range(len(extent))])
    return level


def gaussian(rng, dims, spread, limit, pieces=(), kind=jnp.bfloat16):
    values = jax.random.normal(rng, dims, jnp.float32) * spread
    if len(pieces) > 0:
        values = block_levels(rng, dims, pieces, -0.22, 0.18) * values
    return jnp.clip(values, min=-limit, max=limit).astype(kind)


def setup_inputs(seed: int = 0) -> dict:
    key_list = jax.random.split(jax.random.key(seed), 13)
    return {
        "hidden_in": draw_hidden_in(jax.random.fold_in(key_list[12], 71), 0),
        "key_cache": draw_key_cache(jax.random.fold_in(key_list[12], 71), 0),
        "value_cache": gaussian(key_list[2], (ROWS, KVH, CACHE, HD), 1.0, 6.0, ((0, 32), (1, 8))),
        "query_weight": gaussian(key_list[3], (D, HQ * HD), D ** -0.5, 0.078125, ((1, 8),)),
        "key_weight": gaussian(key_list[4], (D, KVH * HD), D ** -0.5, 0.078125, ((1, 8),)),
        "value_weight": gaussian(key_list[5], (D, KVH * HD), D ** -0.5, 0.078125, ((1, 8),)),
        "output_weight": gaussian(key_list[6], (HQ * HD, D), (GROUP * HD) ** -0.5, 0.3125, ((0, 8),)),
        "norm_gain": jnp.clip(1.0 + 0.18 * jax.random.normal(key_list[7], (D,), jnp.float32), 0.099609375, 1.8984375).astype(jnp.bfloat16),
        "countdown_table": gaussian(key_list[8], (COUNT_TOKENS, D), 0.5, 3.0),
        "countdown_ids": with_ends(jax.random.randint(key_list[9], (STEPS, ROWS), 0, COUNT_TOKENS), jax.random.fold_in(key_list[9], 1), 0, COUNT_TOKENS - 1).astype(jnp.int32),
        "lengths": draw_lengths(jax.random.fold_in(key_list[12], 71), 0),
        "source_slot": draw_source_slot(jax.random.fold_in(key_list[12], 71), 0),
    }


THETA = 1000000.0
EPSILON = 1e-06

def rotate(values, positions):
    half_size = values.shape[-1] // 2
    frequency = THETA ** (-jnp.arange(half_size, dtype=jnp.float32) * 2.0 / values.shape[-1])
    angles = positions.astype(jnp.float32)[:, None] * frequency[None, :]
    cosine = jnp.cos(angles)
    sines = jnp.sin(angles)
    cosine = jnp.concatenate([cosine, cosine], -1)[:, None, :]
    sines = jnp.concatenate([sines, sines], -1)[:, None, :]
    front_half = values[..., :half_size]
    back_half = values[..., half_size:]
    turned = jnp.concatenate([-back_half, front_half], -1)
    return values * cosine + turned * sines

def reference(hidden_in, key_cache, value_cache, query_weight, key_weight, value_weight, output_weight, norm_gain, countdown_table, countdown_ids, lengths, source_slot):
    hidden = hidden_in
    cached_keys = key_cache
    cached_values = value_cache
    current = lengths
    positions = jnp.arange(CACHE, dtype=jnp.int32)
    results = []
    for step_index in range(STEPS):
        source = source_slot[step_index]
        hidden = hidden[source]
        cached_keys = cached_keys[source]
        cached_values = cached_values[source]
        current = current[source]
        mixture = hidden.astype(jnp.float32) + countdown_table[countdown_ids[step_index]].astype(jnp.float32)
        inverse_rms = lax.rsqrt(lax.optimization_barrier(jnp.mean(mixture * mixture, axis=-1, keepdims=True)) + EPSILON)
        normed = (mixture * inverse_rms * norm_gain.astype(jnp.float32)).astype(jnp.bfloat16)
        queries = jnp.dot(normed, query_weight, preferred_element_type=jnp.float32).reshape(ROWS, KVH * GROUP, HD)
        fresh_key = jnp.dot(normed, key_weight, preferred_element_type=jnp.float32).reshape(ROWS, KVH, HD)
        fresh_value = jnp.dot(normed, value_weight, preferred_element_type=jnp.float32).reshape(ROWS, KVH, HD)
        queries = rotate(queries, current).astype(jnp.bfloat16).reshape(ROWS, KVH, GROUP, HD)
        fresh_key = rotate(fresh_key, current).astype(jnp.bfloat16)
        fresh_value = fresh_value.astype(jnp.bfloat16)
        chosen = (positions[None, :] == current[:, None])[:, None, :, None]
        cached_keys = jnp.where(chosen, fresh_key[:, :, None, :], cached_keys)
        cached_values = jnp.where(chosen, fresh_value[:, :, None, :], cached_values)
        scores = jnp.einsum('rhgd,rhcd->rhgc', queries.astype(jnp.float32), cached_keys.astype(jnp.float32)) * HD ** (-0.5)
        allowed = (positions[None, :] <= current[:, None])[:, None, None, :]
        scores = jnp.where(allowed, scores, -jnp.inf)
        highest = lax.optimization_barrier(jnp.max(scores, axis=-1, keepdims=True))
        weights = jnp.exp(scores - highest)
        weights = (weights / lax.optimization_barrier(jnp.sum(weights, axis=-1, keepdims=True))).astype(jnp.bfloat16)
        attended = jnp.einsum('rhgc,rhcd->rhgd', weights.astype(jnp.float32), cached_values.astype(jnp.float32))
        attended = attended.astype(jnp.bfloat16).reshape(ROWS, KVH * GROUP * HD)
        update = jnp.dot(attended, output_weight, preferred_element_type=jnp.float32)
        hidden = (mixture + update).astype(jnp.bfloat16)
        results.append(hidden)
        current = current + 1
    return jnp.stack(results)
```

```python
import functools
import math

import jax
import jax.numpy as jnp
from jax import lax
from jax.experimental import pallas as pl
from jax.experimental.pallas import tpu as pltpu
from jax.sharding import PartitionSpec as P

MESH = pl.DeviceIdType.MESH
F32 = jnp.float32
BF16 = jnp.bfloat16
THETA = 1000000.0
EPSILON = 1e-06
LANES = 128
MOVE = 2
KEEP = 4


def iota(shape, dim):
    return lax.broadcasted_iota(jnp.int32, shape, dim)


def ones_at(mask):
    return jnp.where(mask, 1.0, 0.0).astype(F32)


def lane_pick(index, row):
    lanes = iota((index.shape[0], row.shape[1]), 1)
    return jnp.sum(jnp.where(lanes == index, row, 0.0), axis=1, keepdims=True).astype(jnp.int32)


def pack(x):
    rows, width = x.shape
    high = (width // LANES + 1) // 2 * LANES
    low = jnp.concatenate([x[:, high:], jnp.zeros((rows, 2 * high - width), x.dtype)], axis=1)
    return jnp.concatenate([x[:, :high], low], axis=0).astype(BF16)


def unpack(y, width):
    y = y.astype(F32)
    rows, high = y.shape[0] // 2, y.shape[1]
    return jnp.concatenate([y[:rows], y[rows:, : width - high]], axis=1)


def stack_groups(x):
    return jnp.concatenate(
        [x[:, c : c + LANES] for c in range(0, x.shape[1], LANES)], axis=0
    )


def spread_groups(x, rows):
    return jnp.concatenate([x[c : c + rows] for c in range(0, x.shape[0], rows)], axis=1)


def dot(a, b):
    return jnp.dot(a, b, preferred_element_type=F32)


def kernel(
    reps,
    tps,
    hid_hbm,
    keys_hbm,
    values_hbm,
    wq_hbm,
    wk_hbm,
    wv_hbm,
    wo_hbm,
    gain_hbm,
    table_hbm,
    ids_hbm,
    len_hbm,
    src_hbm,
    out_hbm,
    hid_v,
    keys_v,
    values_v,
    wqkv_v,
    wo_v,
    gain_v,
    table_v,
    ids_v,
    len_s,
    src_v,
    gains_v,
    wide_v,
    sums_v,
    tab_v,
    rank_v,
    first_v,
    last_v,
    id_send,
    id_recv,
    part_send,
    part_recv,
    home_buf,
    first_buf,
    last_buf,
    row_send,
    row_recv,
    att_send,
    att_recv,
    load_sem,
    weight_sem,
    out_w_sem,
    id_ssem,
    id_rsem,
    part_ssem,
    part_rsem,
    gath_ssem,
    gath_rsem,
    row_ssem,
    row_rsem,
    att_ssem,
    att_rsem,
    out_sem,
):
    r = lax.axis_index("rep")
    t = lax.axis_index("tp")
    rows = hid_v.shape[0]
    chunk = wo_v.shape[2]
    groups = chunk // LANES
    heads = wo_v.shape[1] // LANES
    qcols = heads * LANES
    total_rows = rows * reps
    capacity = keys_v.shape[1]
    tokens = table_v.shape[1]
    model = chunk * tps
    half = LANES // 2
    erows = row_send.shape[0]
    arows = att_send.shape[0]

    def chunk_cols(c):
        return pl.ds(pl.multiple_of(c * chunk, LANES), chunk)

    def chunk_rows(c):
        return pl.ds(pl.multiple_of(c * chunk, LANES), chunk)

    small = [
        pltpu.make_async_copy(src_hbm, src_v, load_sem.at[0]),
        pltpu.make_async_copy(ids_hbm, ids_v, load_sem.at[1]),
        pltpu.make_async_copy(len_hbm, len_s, load_sem.at[2]),
        pltpu.make_async_copy(hid_hbm, hid_v, load_sem.at[3]),
        pltpu.make_async_copy(gain_hbm, gain_v, load_sem.at[4]),
    ]
    for copy in small:
        copy.start()

    def table_copy(c):
        return pltpu.make_async_copy(
            table_hbm.at[:, chunk_cols(c)], table_v.at[c], load_sem.at[7 + c]
        )

    for c in range(tps):
        table_copy(c).start()

    def weight_copies(c):
        return [
            pltpu.make_async_copy(
                wq_hbm.at[chunk_rows(c), :], wqkv_v.at[c, :, pl.ds(0, qcols)], weight_sem.at[0, c]
            ),
            pltpu.make_async_copy(
                wk_hbm.at[chunk_rows(c), :], wqkv_v.at[c, :, pl.ds(qcols, LANES)], weight_sem.at[1, c]
            ),
            pltpu.make_async_copy(
                wv_hbm.at[chunk_rows(c), :],
                wqkv_v.at[c, :, pl.ds(qcols + LANES, LANES)],
                weight_sem.at[2, c],
            ),
        ]

    @pl.loop(0, tps)
    def _(c):
        for copy in weight_copies(c):
            copy.start()

    cache_copies = [
        pltpu.make_async_copy(keys_hbm, keys_v, load_sem.at[5]),
        pltpu.make_async_copy(values_hbm, values_v, load_sem.at[6]),
    ]
    for copy in cache_copies:
        copy.start()

    def out_weight_copy(c):
        return pltpu.make_async_copy(wo_hbm.at[:, chunk_cols(c)], wo_v.at[c], out_w_sem.at[c])

    @pl.loop(0, tps)
    def _(c):
        out_weight_copy(c).start()

    barrier = pltpu.get_barrier_semaphore()

    @pl.loop(1, reps)
    def _(d):
        pl.semaphore_signal(
            barrier, inc=1, device_id=(lax.rem(r + d, reps), t), device_id_type=MESH
        )

    @pl.loop(1, tps)
    def _(d):
        pl.semaphore_signal(
            barrier, inc=1, device_id=(r, lax.rem(t + d, tps)), device_id_type=MESH
        )

    small[1].wait()
    id_send[...] = jnp.zeros_like(id_send)
    id_send[:, 0:rows] = ids_v[...]
    pl.semaphore_wait(barrier, reps + tps - 2)

    def to_all_reps(src, dst, send_sem, recv_sem):
        @pl.loop(1, reps)
        def _(d):
            pltpu.make_async_remote_copy(
                src_ref=src,
                dst_ref=dst.at[r],
                send_sem=send_sem,
                recv_sem=recv_sem,
                device_id=(lax.rem(r + d, reps), t),
                device_id_type=MESH,
            ).start()

    def wait_reps(dst, sem):
        blocks = dst.at[pl.ds(0, reps - 1)]
        pltpu.make_async_copy(blocks, blocks, sem).wait()

    to_all_reps(id_send, id_recv, id_ssem, id_rsem)
    id_recv[r] = id_send[...]

    small[0].wait()
    src0 = src_v[0:1, :].astype(F32)
    src1 = src_v[1:2, :].astype(F32)
    square = (total_rows, total_rows)
    subs, lanes = iota(square, 0), iota(square, 1)
    far = (subs >> 3) != (lanes >> 3)
    subs_f = subs.astype(F32)
    slot0 = ones_at(src0 == subs_f)
    slot1 = ones_at(src1 == subs_f)
    both = dot(slot0.astype(BF16), slot1.astype(BF16))
    leaves = jnp.where(far, slot0 + both, 0.0).astype(BF16)
    moved = ones_at(dot(leaves, jnp.ones((total_rows, LANES), BF16)) > 0.5)
    before = ones_at(((subs >> 3) == (lanes >> 3)) & (lanes < subs)).astype(BF16)
    rank = dot(before, moved.astype(BF16))
    rank_v[...] = jnp.where(moved > 0.5, rank, float(rows))

    row_of = iota((rows, total_rows), 0) + r * rows
    glanes = iota((rows, total_rows), 1)
    glanes_f = glanes.astype(F32)
    to0 = jnp.sum(jnp.where(src0 == row_of.astype(F32), glanes_f, 0.0), axis=1, keepdims=True)
    to1 = jnp.sum(jnp.where(src1 == to0, glanes_f, 0.0), axis=1, keepdims=True)
    to0, to1 = to0.astype(jnp.int32), to1.astype(jnp.int32)

    own_rank = rank_v[pl.ds(pl.multiple_of(r * rows, rows), rows), :]
    diagonal = iota((rows, LANES), 0) == (iota((rows, LANES), 1) & (rows - 1))
    rank_lane = jnp.sum(jnp.where(diagonal, own_rank, 0.0), axis=0, keepdims=True)

    def gather_sent(sent, kinds):
        shape = (sent, kinds * rows)
        p, q = iota(shape, 0), iota(shape, 1)
        want = (p & (KEEP - 1)).astype(F32)
        hit = ((p >> 2) == (q >> 3)) & (rank_lane[:, : kinds * rows] == want)
        return ones_at(hit).astype(BF16)

    row_pick = gather_sent(erows, groups)
    att_pick = gather_sent(arows, heads)

    def take_slots(kinds, sent, final):
        count = kinds * rows
        slot = r * rows + (iota((count, 1), 0) & (rows - 1))
        if final:
            slot = lane_pick(slot, src1)
        row = lane_pick(slot, src0)
        kind = iota((count, 1), 0) >> 3
        home = row >> 3
        one = ones_at(iota((count, total_rows), 1) == row).astype(BF16)
        k = dot(one, rank_v[...].astype(BF16)).astype(jnp.int32)[:, 0:1]
        far_at = jnp.where(home == r, -1, home * sent + kind * KEEP + k)
        near_at = jnp.where(home == r, kind * rows + (row & (rows - 1)), -1)
        from_far = ones_at(iota((count, reps * sent), 1) == far_at).astype(BF16)
        from_near = ones_at(iota((count, count), 1) == near_at).astype(BF16)
        return from_far, from_near

    first_far, first_near = take_slots(groups, erows, False)
    last_far, last_near = take_slots(groups, erows, True)
    att_far, att_near = take_slots(heads, arows, True)

    small[2].wait()
    sub8 = iota((rows, 1), 0)
    position = jnp.zeros((rows, 1), jnp.int32)
    for i in range(rows):
        position = jnp.where(sub8 == i, len_s[r * rows + i], position)
    lane128 = iota((1, LANES), 1)
    exponent = (lane128 & (half - 1)).astype(F32) * (-2.0 / LANES)
    frequency = jnp.exp(exponent * math.log(THETA))
    sign = jnp.where(lane128 < half, -1.0, 1.0)

    def turns(place):
        angles = place.astype(F32) * frequency
        return jnp.cos(angles), jnp.sin(angles) * sign

    token_lane = iota((rows, tokens), 1)

    def token_pick(ids):
        return ones_at(token_lane == ids)

    def hidden_chunk(c):
        return hid_v[:, chunk_cols(c)].astype(F32)

    lane8 = iota((rows, LANES), 1)

    def local_pick(step, slot):
        mine = jnp.where(lane8 == slot, id_send[step : step + 1, :].astype(F32), 0.0)
        return token_pick(jnp.sum(mine, axis=1, keepdims=True).astype(jnp.int32))

    stay_pick = local_pick(0, to0 & (rows - 1)).astype(BF16)
    slot_pick = local_pick(1, sub8)
    leaves0 = ones_at((to0 >> 3) != r)
    earlier = ones_at(iota((rows, rows), 1) < iota((rows, rows), 0)).astype(BF16)
    order = dot(earlier, jnp.broadcast_to(leaves0, (rows, LANES)).astype(BF16))[:, 0:1]
    movers = [(leaves0 > 0.5) & (order == float(k)) for k in range(MOVE)]
    for copy in small[3:]:
        copy.wait()
    gain = gain_v[...].astype(F32).reshape(1, model)
    for c in range(tps):
        table_copy(c).wait()
        gains_v[c] = jnp.broadcast_to(gain[:, c * chunk : (c + 1) * chunk], (rows, chunk))

    def gain_chunk(c):
        return gains_v[c, 0:1, :]

    def squares_of(mixture):
        sq = mixture * mixture
        return sum(sq[:, g * LANES : (g + 1) * LANES] for g in range(groups))

    def project(c, mixture, carry):
        acc, squares = carry
        scaled = (mixture * gain_chunk(c)).astype(BF16)
        return acc + dot(scaled, wqkv_v[c]), squares + squares_of(mixture)

    def normalise(carry):
        acc, squares = carry
        mean = jnp.sum(squares, axis=1, keepdims=True) * (1.0 / model)
        return acc * lax.rsqrt(mean + EPSILON)

    zero_carry = (jnp.zeros((rows, qcols + 2 * LANES), F32), jnp.zeros((rows, LANES), F32))
    cap_lane = iota((rows, capacity), 1)
    scale = LANES**-0.5

    def round16(x):
        return x.astype(BF16).astype(F32)

    def attend(qkv, place, fresh):
        cosine, sine = turns(place)

        def rotate(x):
            return round16(x * cosine + pltpu.roll(x, half, 1) * sine)

        queries = [rotate(qkv[:, h * LANES : (h + 1) * LANES]) for h in range(heads)]
        fresh_key = rotate(qkv[:, qcols : qcols + LANES])
        fresh_value = round16(qkv[:, qcols + LANES :])
        fresh = fresh + [(fresh_key, fresh_value, place)]
        stacked = jnp.concatenate(queries, axis=0).astype(BF16)
        scores = [jnp.zeros((rows, capacity), F32)] * heads
        for i in range(rows):
            one = lax.dot_general(
                stacked, keys_v[i], (((1,), (1,)), ((), ())), preferred_element_type=F32
            )
            for h in range(heads):
                scores[h] = jnp.where(sub8 == i, one[h * rows : (h + 1) * rows], scores[h])
        weights, extra = [], []
        for h in range(heads):
            s = scores[h] * scale
            news = [jnp.sum(queries[h] * k, axis=1, keepdims=True) * scale for k, _, _ in fresh]
            for new, (_, _, at) in zip(news, fresh):
                s = jnp.where(cap_lane == at, new, s)
            s = jnp.where(cap_lane <= place, s, -jnp.inf)
            top = jnp.max(s, axis=1, keepdims=True)
            e = jnp.exp(s - top)
            total = jnp.sum(e, axis=1, keepdims=True)
            w = e / total
            for _, _, at in fresh:
                w = jnp.where(cap_lane == at, 0.0, w)
            weights.append(w)
            extra.append([round16(jnp.exp(new - top) / total) for new in news])
        stacked = jnp.concatenate(weights, axis=0).astype(BF16)
        outs = [jnp.zeros((rows, LANES), F32)] * heads
        for i in range(rows):
            one = dot(stacked, values_v[i])
            for h in range(heads):
                outs[h] = jnp.where(sub8 == i, one[h * rows : (h + 1) * rows], outs[h])
        for h in range(heads):
            for w, (_, v, _) in zip(extra[h], fresh):
                outs[h] = outs[h] + w * v
        return jnp.concatenate(outs, axis=0).astype(BF16), fresh

    def part_copy(step, to, src):
        return pltpu.make_async_remote_copy(
            src_ref=part_send.at[step, to],
            dst_ref=part_recv.at[step, src],
            send_sem=part_ssem.at[step, to],
            recv_sem=part_rsem.at[step, src],
            device_id=(r, to),
            device_id_type=MESH,
        )

    def far_first(n):
        odd = lax.rem(n, 2)
        return tps // 2 + (lax.div(n, 2) + odd) * (1 - 2 * odd)

    def output_sum(step, attended, wait_weights, meanwhile):
        @pl.loop(0, tps - 1)
        def _(n):
            to = lax.rem(t + far_first(n), tps)
            if wait_weights:
                out_weight_copy(to).wait()
            part_send[step, to] = pack(dot(attended, wo_v[to]))
            part_copy(step, to, t).start()

        if wait_weights:
            out_weight_copy(t).wait()
        total = dot(attended, wo_v[t])
        meanwhile()

        def add(d, total):
            src = lax.rem(t + d, tps)
            part_copy(step, t, src).wait_recv()
            return total + unpack(part_recv[step, src], chunk)

        return lax.fori_loop(1, tps, add, total)

    def gather_copy(which, buf, to, src):
        return pltpu.make_async_remote_copy(
            src_ref=buf.at[src],
            dst_ref=buf.at[src],
            send_sem=gath_ssem.at[which, to],
            recv_sem=gath_rsem.at[which, src],
            device_id=(r, to),
            device_id_type=MESH,
        )

    def gather_start(which, buf, block):
        buf[t] = block

        @pl.loop(0, tps - 1)
        def _(n):
            gather_copy(which, buf, lax.rem(t + far_first(n), tps), t).start()

    sums_v[...] = jnp.zeros_like(sums_v)
    wide_v[...] = jnp.zeros_like(wide_v)

    @pl.loop(0, tps)
    def _(c):
        for copy in weight_copies(c):
            copy.wait()
        hid = hidden_chunk(c)
        table = table_v[c]
        blocks = [hid + dot(stay_pick, table)]
        for mover in movers:
            row = jnp.sum(jnp.where(mover, hid, 0.0), axis=0, keepdims=True)
            blocks.append(row + table.astype(F32))
        mixture = jnp.concatenate(blocks, axis=0)
        wide_v[...] += dot((mixture * gain_chunk(c)).astype(BF16), wqkv_v[c])
        sums_v[...] += squares_of(mixture)

    wait_reps(id_recv, id_rsem)
    id_rows = [jnp.zeros((rows, LANES), F32), jnp.zeros((rows, LANES), F32)]
    for h in range(reps):
        block = id_recv[h].astype(F32)
        for step, slot in enumerate((to0, to1)):
            id_rows[step] = jnp.where((slot >> 3) == h, block[step : step + 1, :], id_rows[step])
    ids = []
    for step, slot in enumerate((to0, to1)):
        mine = jnp.where(lane8 == (slot & (rows - 1)), id_rows[step], 0.0)
        ids.append(jnp.sum(mine, axis=1, keepdims=True))
    now_pick, next_pick = [token_pick(i.astype(jnp.int32)) for i in ids]
    carry = wide_v[0:rows, :], sums_v[0:rows, :]
    token_sub = iota((tokens, 1), 0).astype(F32)
    for k, mover in enumerate(movers):
        token = jnp.sum(jnp.where(mover, ids[0], 0.0), axis=0, keepdims=True)
        at = slice(rows + k * tokens, rows + (k + 1) * tokens)
        carry = tuple(
            jnp.where(
                mover,
                jnp.sum(jnp.where(token_sub == token, wide[at, :], 0.0), axis=0, keepdims=True),
                kept,
            )
            for wide, kept in zip((wide_v, sums_v), carry)
        )
    qkv = normalise(carry)
    for copy in cache_copies:
        copy.wait()
    attended, fresh = attend(qkv, position, [])
    attended = spread_groups(attended, rows)

    def find_tokens():
        picks = jnp.concatenate([next_pick, slot_pick], axis=0).astype(BF16)
        for c in range(tps):
            tab_v[c] = dot(picks, table_v[c])
        mix.append(hidden_chunk(t) + dot(now_pick.astype(BF16), table_v[t]))

    mix = []
    summed = output_sum(0, attended, True, find_tokens)
    hidden = round16(mix[0] + summed)
    gather_start(0, home_buf, pack(hidden))
    own_groups = stack_groups(hidden).astype(BF16)
    row_send[...] = dot(row_pick, own_groups).astype(BF16)
    to_all_reps(row_send, row_recv, row_ssem, row_rsem)
    row_recv[r] = row_send[...]

    carry = project(t, hidden + tab_v[t, 0:rows], zero_carry)

    def next_project(n, carry):
        src = lax.rem(t + far_first(tps - 2 - n), tps)
        gather_copy(0, home_buf, t, src).wait_recv()
        return project(src, unpack(home_buf[src], chunk) + tab_v[src, 0:rows], carry)

    qkv = normalise(lax.fori_loop(0, tps - 1, next_project, carry))

    attended, _ = attend(qkv, position + 1, fresh)
    att_send[...] = dot(att_pick, attended).astype(BF16)
    to_all_reps(att_send, att_recv, att_ssem, att_rsem)
    att_recv[r] = att_send[...]

    wait_reps(row_recv, row_rsem)
    received = row_recv[...].reshape(reps * erows, LANES)
    first = spread_groups(dot(first_far, received) + dot(first_near, own_groups), rows)
    last = spread_groups(dot(last_far, received) + dot(last_near, own_groups), rows)
    last = last + tab_v[t, rows:]
    gather_start(1, first_buf, pack(first))

    wait_reps(att_recv, att_rsem)
    received = att_recv[...].reshape(reps * arows, LANES)
    attended = (dot(att_far, received) + dot(att_near, attended)).astype(BF16)
    attended = spread_groups(attended, rows)

    def result(which, buf, out_v):
        @pl.loop(1, tps)
        def _(d):
            gather_copy(which, buf, t, lax.rem(t + d, tps)).wait_recv()

        for c in range(tps):
            cols = slice(c * chunk, (c + 1) * chunk)
            out_v[:, cols] = unpack(buf[c], chunk).astype(BF16)
        copy = pltpu.make_async_copy(out_v, out_hbm.at[which - 1], out_sem.at[which - 1])
        copy.start()
        return copy

    outs = []
    summed = output_sum(1, attended, False, lambda: outs.append(result(1, first_buf, first_v)))
    hidden = last + summed
    gather_start(2, last_buf, pack(hidden))
    outs.append(result(2, last_buf, last_v))

    wait_reps(id_recv, id_ssem)
    wait_reps(row_recv, row_ssem)
    wait_reps(att_recv, att_ssem)

    @pl.loop(1, tps)
    def _(d):
        to = lax.rem(t + d, tps)
        for step in range(2):
            part_copy(step, to, t).wait_send()
        for which, buf in enumerate((home_buf, first_buf, last_buf)):
            gather_copy(which, buf, to, t).wait_send()

    for copy in outs:
        copy.wait()


def body(
    reps,
    tps,
    hidden_in,
    key_cache,
    value_cache,
    query_weight,
    key_weight,
    value_weight,
    output_weight,
    norm_gain,
    countdown_table,
    countdown_ids,
    lengths,
    source_slot,
):
    rows, model = hidden_in.shape
    capacity, head = key_cache.shape[2:]
    chunk = model // tps
    qcols = query_weight.shape[1]
    heads = qcols // head
    tokens = countdown_table.shape[0]
    steps = countdown_ids.shape[0]
    total_rows = lengths.shape[0]
    groups = chunk // LANES
    high = (groups + 1) // 2 * LANES
    erows = -(-groups * KEEP // 16) * 16
    arows = -(-heads * KEEP // 16) * 16
    block = (2 * rows, high)
    dma, vmem = pltpu.SemaphoreType.DMA, pltpu.VMEM
    scratch = [
        vmem((rows, model), BF16),
        vmem((rows, capacity, head), BF16),
        vmem((rows, capacity, head), BF16),
        vmem((tps, chunk, qcols + 2 * head), BF16),
        vmem((tps, qcols, chunk), BF16),
        vmem((model,), BF16),
        vmem((tps, tokens, chunk), BF16),
        vmem((steps, rows), jnp.int32),
        pltpu.SMEM((total_rows,), jnp.int32),
        vmem((steps, total_rows), jnp.int32),
        vmem((tps, rows, chunk), F32),
        vmem((rows + MOVE * tokens, qcols + 2 * head), F32),
        vmem((rows + MOVE * tokens, LANES), F32),
        vmem((tps, 2 * rows, chunk), F32),
        vmem((total_rows, LANES), F32),
        vmem((rows, model), BF16),
        vmem((rows, model), BF16),
        vmem((steps, LANES), jnp.int32),
        vmem((reps, steps, LANES), jnp.int32),
        vmem((steps, tps) + block, BF16),
        vmem((steps, tps) + block, BF16),
        vmem((tps,) + block, BF16),
        vmem((tps,) + block, BF16),
        vmem((tps,) + block, BF16),
        vmem((erows, LANES), BF16),
        vmem((reps, erows, LANES), BF16),
        vmem((arows, LANES), BF16),
        vmem((reps, arows, LANES), BF16),
        dma((7 + tps,)),
        dma((3, tps)),
        dma((tps,)),
        dma,
        dma,
        dma((steps, tps)),
        dma((steps, tps)),
        dma((3, tps)),
        dma((3, tps)),
        dma,
        dma,
        dma,
        dma,
        dma((2,)),
    ]
    return pl.pallas_call(
        functools.partial(kernel, reps, tps),
        out_shape=jax.ShapeDtypeStruct((steps, rows, model), BF16),
        in_specs=[pl.BlockSpec(memory_space=pl.ANY)] * 12,
        out_specs=pl.BlockSpec(memory_space=pl.ANY),
        scratch_shapes=scratch,
        compiler_params=pltpu.CompilerParams(
            collective_id=0, has_side_effects=True, vmem_limit_bytes=60 * 2**20
        ),
    )(
        hidden_in,
        key_cache.reshape(rows, capacity, head),
        value_cache.reshape(rows, capacity, head),
        query_weight,
        key_weight,
        value_weight,
        output_weight,
        norm_gain,
        countdown_table,
        countdown_ids,
        lengths,
        source_slot,
    )


def solution(mesh):
    placed = (
        P("rep", None),
        P("rep", "tp", None, None),
        P("rep", "tp", None, None),
        P(None, "tp"),
        P(None, "tp"),
        P(None, "tp"),
        P("tp", None),
        P(),
        P(),
        P(None, "rep"),
        P(),
        P(),
    )
    return jax.shard_map(
        functools.partial(body, mesh.shape["rep"], mesh.shape["tp"]),
        mesh=mesh,
        in_specs=placed,
        out_specs=P(None, "rep", None),
        check_vma=False,
    )
```

```python
import functools
import math

import jax
import jax.numpy as jnp
from jax import lax
from jax.experimental import pallas as pl
from jax.experimental.pallas import tpu as pltpu
from jax.sharding import PartitionSpec as P

MESH = pl.DeviceIdType.MESH
F32 = jnp.float32
BF16 = jnp.bfloat16
THETA = 1000000.0
EPSILON = 1e-06
LANES = 128
MOVE = 2
KEEP = 4


def iota(shape, dim):
    return lax.broadcasted_iota(jnp.int32, shape, dim)


def ones_at(mask):
    return jnp.where(mask, 1.0, 0.0).astype(F32)


def lane_pick(index, row):
    lanes = iota((index.shape[0], row.shape[1]), 1)
    return jnp.sum(jnp.where(lanes == index, row, 0.0), axis=1, keepdims=True).astype(jnp.int32)


def pack(x):
    rows, width = x.shape
    high = (width // LANES + 1) // 2 * LANES
    low = jnp.concatenate([x[:, high:], jnp.zeros((rows, 2 * high - width), x.dtype)], axis=1)
    return jnp.concatenate([x[:, :high], low], axis=0).astype(BF16)


def unpack(y, width):
    y = y.astype(F32)
    rows, high = y.shape[0] // 2, y.shape[1]
    return jnp.concatenate([y[:rows], y[rows:, : width - high]], axis=1)


def stack_groups(x):
    return jnp.concatenate(
        [x[:, c : c + LANES] for c in range(0, x.shape[1], LANES)], axis=0
    )


def spread_groups(x, rows):
    return jnp.concatenate([x[c : c + rows] for c in range(0, x.shape[0], rows)], axis=1)


def dot(a, b):
    return jnp.dot(a, b, preferred_element_type=F32)


def kernel(
    reps,
    tps,
    hid_hbm,
    keys_hbm,
    values_hbm,
    wq_hbm,
    wk_hbm,
    wv_hbm,
    wo_hbm,
    gain_hbm,
    table_hbm,
    ids_hbm,
    len_hbm,
    src_hbm,
    out_hbm,
    hid_v,
    keys_v,
    values_v,
    wqkv_v,
    wo_v,
    gain_v,
    table_v,
    ids_v,
    len_s,
    src_v,
    gains_v,
    wide_v,
    sums_v,
    tab_v,
    rank_v,
    first_v,
    last_v,
    id_send,
    id_recv,
    part_send,
    part_recv,
    home_buf,
    first_buf,
    last_buf,
    row_send,
    row_recv,
    att_send,
    att_recv,
    load_sem,
    weight_sem,
    out_w_sem,
    id_ssem,
    id_rsem,
    part_ssem,
    part_rsem,
    gath_ssem,
    gath_rsem,
    row_ssem,
    row_rsem,
    att_ssem,
    att_rsem,
    out_sem,
):
    r = lax.axis_index("rep")
    t = lax.axis_index("tp")
    rows = hid_v.shape[0]
    chunk = wo_v.shape[2]
    groups = chunk // LANES
    heads = wo_v.shape[1] // LANES
    qcols = heads * LANES
    total_rows = rows * reps
    capacity = keys_v.shape[1]
    tokens = table_v.shape[1]
    model = chunk * tps
    half = LANES // 2
    erows = row_send.shape[0]
    arows = att_send.shape[0]

    def chunk_cols(c):
        return pl.ds(pl.multiple_of(c * chunk, LANES), chunk)

    def chunk_rows(c):
        return pl.ds(pl.multiple_of(c * chunk, LANES), chunk)

    small = [
        pltpu.make_async_copy(src_hbm, src_v, load_sem.at[0]),
        pltpu.make_async_copy(ids_hbm, ids_v, load_sem.at[1]),
        pltpu.make_async_copy(len_hbm, len_s, load_sem.at[2]),
        pltpu.make_async_copy(hid_hbm, hid_v, load_sem.at[3]),
        pltpu.make_async_copy(gain_hbm, gain_v, load_sem.at[4]),
    ]
    for copy in small:
        copy.start()

    def table_copy(c):
        return pltpu.make_async_copy(
            table_hbm.at[:, chunk_cols(c)], table_v.at[c], load_sem.at[7 + c]
        )

    for c in range(tps):
        table_copy(c).start()

    def weight_copies(c):
        return [
            pltpu.make_async_copy(
                wq_hbm.at[chunk_rows(c), :], wqkv_v.at[c, :, pl.ds(0, qcols)], weight_sem.at[0, c]
            ),
            pltpu.make_async_copy(
                wk_hbm.at[chunk_rows(c), :], wqkv_v.at[c, :, pl.ds(qcols, LANES)], weight_sem.at[1, c]
            ),
            pltpu.make_async_copy(
                wv_hbm.at[chunk_rows(c), :],
                wqkv_v.at[c, :, pl.ds(qcols + LANES, LANES)],
                weight_sem.at[2, c],
            ),
        ]

    @pl.loop(0, tps)
    def _(c):
        for copy in weight_copies(c):
            copy.start()

    cache_copies = [
        pltpu.make_async_copy(keys_hbm, keys_v, load_sem.at[5]),
        pltpu.make_async_copy(values_hbm, values_v, load_sem.at[6]),
    ]
    for copy in cache_copies:
        copy.start()

    def out_weight_copy(c):
        return pltpu.make_async_copy(wo_hbm.at[:, chunk_cols(c)], wo_v.at[c], out_w_sem.at[c])

    @pl.loop(0, tps)
    def _(c):
        out_weight_copy(c).start()

    def far_first(n):
        odd = lax.rem(n, 2)
        return tps // 2 + (lax.div(n, 2) + odd) * (1 - 2 * odd)

    sizes = (4, 4, 2) if reps == 32 else (reps,)

    def other_reps(visit):
        def partner(n):
            peer, stride = 0, 1
            for size in reversed(sizes):
                own = lax.rem(lax.div(r, stride), size)
                step = lax.rem(lax.div(n, stride), size) + size // 2
                peer = peer + lax.rem(own + step, size) * stride
                stride *= size
            return peer

        own, stride = 0, 1
        for size in reversed(sizes):
            own, stride = own + (size - size // 2) * stride, stride * size
        for low, high in ((0, own), (own + 1, reps)):

            @pl.loop(low, high)
            def _(n):
                visit(partner(n))

    barrier = pltpu.get_barrier_semaphore()

    def greet(to):
        pl.semaphore_signal(barrier, inc=1, device_id=to, device_id_type=MESH)

    other_reps(lambda peer: greet((peer, t)))

    @pl.loop(0, tps - 1)
    def _(n):
        greet((r, lax.rem(t + far_first(n), tps)))

    small[1].wait()
    id_send[...] = jnp.zeros_like(id_send)
    id_send[:, 0:rows] = ids_v[...]
    pl.semaphore_wait(barrier, reps + tps - 2)

    def to_all_reps(src, dst, send_sem, recv_sem):
        def send(peer):
            pltpu.make_async_remote_copy(
                src_ref=src,
                dst_ref=dst.at[r],
                send_sem=send_sem,
                recv_sem=recv_sem,
                device_id=(peer, t),
                device_id_type=MESH,
            ).start()

        other_reps(send)

    def wait_reps(dst, sem):
        blocks = dst.at[pl.ds(0, reps - 1)]
        pltpu.make_async_copy(blocks, blocks, sem).wait()

    to_all_reps(id_send, id_recv, id_ssem, id_rsem)
    id_recv[r] = id_send[...]

    small[0].wait()
    src0 = src_v[0:1, :].astype(F32)
    src1 = src_v[1:2, :].astype(F32)
    square = (total_rows, total_rows)
    subs, lanes = iota(square, 0), iota(square, 1)
    far = (subs >> 3) != (lanes >> 3)
    subs_f = subs.astype(F32)
    slot0 = ones_at(src0 == subs_f)
    slot1 = ones_at(src1 == subs_f)
    both = dot(slot0.astype(BF16), slot1.astype(BF16))
    leaves = jnp.where(far, slot0 + both, 0.0).astype(BF16)
    moved = ones_at(dot(leaves, jnp.ones((total_rows, LANES), BF16)) > 0.5)
    before = ones_at(((subs >> 3) == (lanes >> 3)) & (lanes < subs)).astype(BF16)
    rank = dot(before, moved.astype(BF16))
    rank_v[...] = jnp.where(moved > 0.5, rank, float(rows))

    row_of = iota((rows, total_rows), 0) + r * rows
    glanes = iota((rows, total_rows), 1)
    glanes_f = glanes.astype(F32)
    to0 = jnp.sum(jnp.where(src0 == row_of.astype(F32), glanes_f, 0.0), axis=1, keepdims=True)
    to1 = jnp.sum(jnp.where(src1 == to0, glanes_f, 0.0), axis=1, keepdims=True)
    to0, to1 = to0.astype(jnp.int32), to1.astype(jnp.int32)

    own_rank = rank_v[pl.ds(pl.multiple_of(r * rows, rows), rows), :]
    diagonal = iota((rows, LANES), 0) == (iota((rows, LANES), 1) & (rows - 1))
    rank_lane = jnp.sum(jnp.where(diagonal, own_rank, 0.0), axis=0, keepdims=True)

    def gather_sent(sent, kinds):
        shape = (sent, kinds * rows)
        p, q = iota(shape, 0), iota(shape, 1)
        want = (p & (KEEP - 1)).astype(F32)
        hit = ((p >> 2) == (q >> 3)) & (rank_lane[:, : kinds * rows] == want)
        return ones_at(hit).astype(BF16)

    row_pick = gather_sent(erows, groups)
    att_pick = gather_sent(arows, heads)

    def take_slots(kinds, sent, final):
        count = kinds * rows
        slot = r * rows + (iota((count, 1), 0) & (rows - 1))
        if final:
            slot = lane_pick(slot, src1)
        row = lane_pick(slot, src0)
        kind = iota((count, 1), 0) >> 3
        home = row >> 3
        one = ones_at(iota((count, total_rows), 1) == row).astype(BF16)
        k = dot(one, rank_v[...].astype(BF16)).astype(jnp.int32)[:, 0:1]
        far_at = jnp.where(home == r, -1, home * sent + kind * KEEP + k)
        near_at = jnp.where(home == r, kind * rows + (row & (rows - 1)), -1)
        from_far = ones_at(iota((count, reps * sent), 1) == far_at).astype(BF16)
        from_near = ones_at(iota((count, count), 1) == near_at).astype(BF16)
        return from_far, from_near

    first_far, first_near = take_slots(groups, erows, False)
    last_far, last_near = take_slots(groups, erows, True)
    att_far, att_near = take_slots(heads, arows, True)

    small[2].wait()
    sub8 = iota((rows, 1), 0)
    position = jnp.zeros((rows, 1), jnp.int32)
    for i in range(rows):
        position = jnp.where(sub8 == i, len_s[r * rows + i], position)
    lane128 = iota((1, LANES), 1)
    exponent = (lane128 & (half - 1)).astype(F32) * (-2.0 / LANES)
    frequency = jnp.exp(exponent * math.log(THETA))
    sign = jnp.where(lane128 < half, -1.0, 1.0)

    def turns(place):
        angles = place.astype(F32) * frequency
        return jnp.cos(angles), jnp.sin(angles) * sign

    token_lane = iota((rows, tokens), 1)

    def token_pick(ids):
        return ones_at(token_lane == ids)

    def hidden_chunk(c):
        return hid_v[:, chunk_cols(c)].astype(F32)

    lane8 = iota((rows, LANES), 1)

    def local_pick(step, slot):
        mine = jnp.where(lane8 == slot, id_send[step : step + 1, :].astype(F32), 0.0)
        return token_pick(jnp.sum(mine, axis=1, keepdims=True).astype(jnp.int32))

    stay_pick = local_pick(0, to0 & (rows - 1)).astype(BF16)
    slot_pick = local_pick(1, sub8)
    leaves0 = ones_at((to0 >> 3) != r)
    earlier = ones_at(iota((rows, rows), 1) < iota((rows, rows), 0)).astype(BF16)
    order = dot(earlier, jnp.broadcast_to(leaves0, (rows, LANES)).astype(BF16))[:, 0:1]
    movers = [(leaves0 > 0.5) & (order == float(k)) for k in range(MOVE)]
    for copy in small[3:]:
        copy.wait()
    gain = gain_v[...].astype(F32).reshape(1, model)
    for c in range(tps):
        table_copy(c).wait()
        gains_v[c] = jnp.broadcast_to(gain[:, c * chunk : (c + 1) * chunk], (rows, chunk))

    def gain_chunk(c):
        return gains_v[c, 0:1, :]

    def squares_of(mixture):
        sq = mixture * mixture
        return sum(sq[:, g * LANES : (g + 1) * LANES] for g in range(groups))

    def project(c, mixture, carry):
        acc, squares = carry
        scaled = (mixture * gain_chunk(c)).astype(BF16)
        return acc + dot(scaled, wqkv_v[c]), squares + squares_of(mixture)

    def normalise(carry):
        acc, squares = carry
        mean = jnp.sum(squares, axis=1, keepdims=True) * (1.0 / model)
        return acc * lax.rsqrt(mean + EPSILON)

    zero_carry = (jnp.zeros((rows, qcols + 2 * LANES), F32), jnp.zeros((rows, LANES), F32))
    cap_lane = iota((rows, capacity), 1)
    scale = LANES**-0.5

    def round16(x):
        return x.astype(BF16).astype(F32)

    def attend(qkv, place, fresh):
        cosine, sine = turns(place)

        def rotate(x):
            return round16(x * cosine + pltpu.roll(x, half, 1) * sine)

        queries = [rotate(qkv[:, h * LANES : (h + 1) * LANES]) for h in range(heads)]
        fresh_key = rotate(qkv[:, qcols : qcols + LANES])
        fresh_value = round16(qkv[:, qcols + LANES :])
        fresh = fresh + [(fresh_key, fresh_value, place)]
        stacked = jnp.concatenate(queries, axis=0).astype(BF16)
        scores = [jnp.zeros((rows, capacity), F32)] * heads
        for i in range(rows):
            one = lax.dot_general(
                stacked, keys_v[i], (((1,), (1,)), ((), ())), preferred_element_type=F32
            )
            for h in range(heads):
                scores[h] = jnp.where(sub8 == i, one[h * rows : (h + 1) * rows], scores[h])
        weights, extra = [], []
        for h in range(heads):
            s = scores[h] * scale
            news = [jnp.sum(queries[h] * k, axis=1, keepdims=True) * scale for k, _, _ in fresh]
            for new, (_, _, at) in zip(news, fresh):
                s = jnp.where(cap_lane == at, new, s)
            s = jnp.where(cap_lane <= place, s, -jnp.inf)
            top = jnp.max(s, axis=1, keepdims=True)
            e = jnp.exp(s - top)
            total = jnp.sum(e, axis=1, keepdims=True)
            w = e / total
            for _, _, at in fresh:
                w = jnp.where(cap_lane == at, 0.0, w)
            weights.append(w)
            extra.append([round16(jnp.exp(new - top) / total) for new in news])
        stacked = jnp.concatenate(weights, axis=0).astype(BF16)
        outs = [jnp.zeros((rows, LANES), F32)] * heads
        for i in range(rows):
            one = dot(stacked, values_v[i])
            for h in range(heads):
                outs[h] = jnp.where(sub8 == i, one[h * rows : (h + 1) * rows], outs[h])
        for h in range(heads):
            for w, (_, v, _) in zip(extra[h], fresh):
                outs[h] = outs[h] + w * v
        return jnp.concatenate(outs, axis=0).astype(BF16), fresh

    def part_copy(step, to, src):
        return pltpu.make_async_remote_copy(
            src_ref=part_send.at[step, to],
            dst_ref=part_recv.at[step, src],
            send_sem=part_ssem.at[step, to],
            recv_sem=part_rsem.at[step, src],
            device_id=(r, to),
            device_id_type=MESH,
        )

    def output_sum(step, attended, wait_weights, meanwhile):
        @pl.loop(0, tps - 1)
        def _(n):
            to = lax.rem(t + far_first(n), tps)
            if wait_weights:
                out_weight_copy(to).wait()
            part_send[step, to] = pack(dot(attended, wo_v[to]))
            part_copy(step, to, t).start()

        if wait_weights:
            out_weight_copy(t).wait()
        total = dot(attended, wo_v[t])
        meanwhile()

        def add(d, total):
            src = lax.rem(t + d, tps)
            part_copy(step, t, src).wait_recv()
            return total + unpack(part_recv[step, src], chunk)

        return lax.fori_loop(1, tps, add, total)

    def gather_copy(which, buf, to, src):
        return pltpu.make_async_remote_copy(
            src_ref=buf.at[src],
            dst_ref=buf.at[src],
            send_sem=gath_ssem.at[which, to],
            recv_sem=gath_rsem.at[which, src],
            device_id=(r, to),
            device_id_type=MESH,
        )

    def gather_start(which, buf, block):
        buf[t] = block

        @pl.loop(0, tps - 1)
        def _(n):
            gather_copy(which, buf, lax.rem(t + far_first(n), tps), t).start()

    sums_v[...] = jnp.zeros_like(sums_v)
    wide_v[...] = jnp.zeros_like(wide_v)

    @pl.loop(0, tps)
    def _(c):
        for copy in weight_copies(c):
            copy.wait()
        hid = hidden_chunk(c)
        table = table_v[c]
        blocks = [hid + dot(stay_pick, table)]
        for mover in movers:
            row = jnp.sum(jnp.where(mover, hid, 0.0), axis=0, keepdims=True)
            blocks.append(row + table.astype(F32))
        mixture = jnp.concatenate(blocks, axis=0)
        wide_v[...] += dot((mixture * gain_chunk(c)).astype(BF16), wqkv_v[c])
        sums_v[...] += squares_of(mixture)

    wait_reps(id_recv, id_rsem)
    id_rows = [jnp.zeros((rows, LANES), F32), jnp.zeros((rows, LANES), F32)]
    for h in range(reps):
        block = id_recv[h].astype(F32)
        for step, slot in enumerate((to0, to1)):
            id_rows[step] = jnp.where((slot >> 3) == h, block[step : step + 1, :], id_rows[step])
    ids = []
    for step, slot in enumerate((to0, to1)):
        mine = jnp.where(lane8 == (slot & (rows - 1)), id_rows[step], 0.0)
        ids.append(jnp.sum(mine, axis=1, keepdims=True))
    now_pick, next_pick = [token_pick(i.astype(jnp.int32)) for i in ids]
    carry = wide_v[0:rows, :], sums_v[0:rows, :]
    token_sub = iota((tokens, 1), 0).astype(F32)
    for k, mover in enumerate(movers):
        token = jnp.sum(jnp.where(mover, ids[0], 0.0), axis=0, keepdims=True)
        at = slice(rows + k * tokens, rows + (k + 1) * tokens)
        carry = tuple(
            jnp.where(
                mover,
                jnp.sum(jnp.where(token_sub == token, wide[at, :], 0.0), axis=0, keepdims=True),
                kept,
            )
            for wide, kept in zip((wide_v, sums_v), carry)
        )
    qkv = normalise(carry)
    for copy in cache_copies:
        copy.wait()
    attended, fresh = attend(qkv, position, [])
    attended = spread_groups(attended, rows)

    def find_tokens():
        picks = jnp.concatenate([next_pick, slot_pick], axis=0).astype(BF16)
        for c in range(tps):
            tab_v[c] = dot(picks, table_v[c])
        mix.append(hidden_chunk(t) + dot(now_pick.astype(BF16), table_v[t]))

    mix = []
    summed = output_sum(0, attended, True, find_tokens)
    hidden = round16(mix[0] + summed)
    gather_start(0, home_buf, pack(hidden))
    own_groups = stack_groups(hidden).astype(BF16)
    row_send[...] = dot(row_pick, own_groups).astype(BF16)
    to_all_reps(row_send, row_recv, row_ssem, row_rsem)
    row_recv[r] = row_send[...]

    carry = project(t, hidden + tab_v[t, 0:rows], zero_carry)

    def next_project(n, carry):
        src = lax.rem(t + far_first(tps - 2 - n), tps)
        gather_copy(0, home_buf, t, src).wait_recv()
        return project(src, unpack(home_buf[src], chunk) + tab_v[src, 0:rows], carry)

    qkv = normalise(lax.fori_loop(0, tps - 1, next_project, carry))

    attended, _ = attend(qkv, position + 1, fresh)
    att_send[...] = dot(att_pick, attended).astype(BF16)
    to_all_reps(att_send, att_recv, att_ssem, att_rsem)
    att_recv[r] = att_send[...]

    wait_reps(row_recv, row_rsem)
    received = row_recv[...].reshape(reps * erows, LANES)
    first = spread_groups(dot(first_far, received) + dot(first_near, own_groups), rows)
    last = spread_groups(dot(last_far, received) + dot(last_near, own_groups), rows)
    last = last + tab_v[t, rows:]
    gather_start(1, first_buf, pack(first))

    wait_reps(att_recv, att_rsem)
    received = att_recv[...].reshape(reps * arows, LANES)
    attended = (dot(att_far, received) + dot(att_near, attended)).astype(BF16)
    attended = spread_groups(attended, rows)

    def result(which, buf, out_v):
        @pl.loop(1, tps)
        def _(d):
            gather_copy(which, buf, t, lax.rem(t + d, tps)).wait_recv()

        for c in range(tps):
            cols = slice(c * chunk, (c + 1) * chunk)
            out_v[:, cols] = unpack(buf[c], chunk).astype(BF16)
        copy = pltpu.make_async_copy(out_v, out_hbm.at[which - 1], out_sem.at[which - 1])
        copy.start()
        return copy

    outs = []
    summed = output_sum(1, attended, False, lambda: outs.append(result(1, first_buf, first_v)))
    hidden = last + summed
    gather_start(2, last_buf, pack(hidden))
    outs.append(result(2, last_buf, last_v))

    wait_reps(id_recv, id_ssem)
    wait_reps(row_recv, row_ssem)
    wait_reps(att_recv, att_ssem)

    @pl.loop(1, tps)
    def _(d):
        to = lax.rem(t + d, tps)
        for step in range(2):
            part_copy(step, to, t).wait_send()
        for which, buf in enumerate((home_buf, first_buf, last_buf)):
            gather_copy(which, buf, to, t).wait_send()

    for copy in outs:
        copy.wait()


def body(
    reps,
    tps,
    hidden_in,
    key_cache,
    value_cache,
    query_weight,
    key_weight,
    value_weight,
    output_weight,
    norm_gain,
    countdown_table,
    countdown_ids,
    lengths,
    source_slot,
):
    rows, model = hidden_in.shape
    capacity, head = key_cache.shape[2:]
    chunk = model // tps
    qcols = query_weight.shape[1]
    heads = qcols // head
    tokens = countdown_table.shape[0]
    steps = countdown_ids.shape[0]
    total_rows = lengths.shape[0]
    groups = chunk // LANES
    high = (groups + 1) // 2 * LANES
    erows = -(-groups * KEEP // 16) * 16
    arows = -(-heads * KEEP // 16) * 16
    block = (2 * rows, high)
    dma, vmem = pltpu.SemaphoreType.DMA, pltpu.VMEM
    scratch = [
        vmem((rows, model), BF16),
        vmem((rows, capacity, head), BF16),
        vmem((rows, capacity, head), BF16),
        vmem((tps, chunk, qcols + 2 * head), BF16),
        vmem((tps, qcols, chunk), BF16),
        vmem((model,), BF16),
        vmem((tps, tokens, chunk), BF16),
        vmem((steps, rows), jnp.int32),
        pltpu.SMEM((total_rows,), jnp.int32),
        vmem((steps, total_rows), jnp.int32),
        vmem((tps, rows, chunk), F32),
        vmem((rows + MOVE * tokens, qcols + 2 * head), F32),
        vmem((rows + MOVE * tokens, LANES), F32),
        vmem((tps, 2 * rows, chunk), F32),
        vmem((total_rows, LANES), F32),
        vmem((rows, model), BF16),
        vmem((rows, model), BF16),
        vmem((steps, LANES), jnp.int32),
        vmem((reps, steps, LANES), jnp.int32),
        vmem((steps, tps) + block, BF16),
        vmem((steps, tps) + block, BF16),
        vmem((tps,) + block, BF16),
        vmem((tps,) + block, BF16),
        vmem((tps,) + block, BF16),
        vmem((erows, LANES), BF16),
        vmem((reps, erows, LANES), BF16),
        vmem((arows, LANES), BF16),
        vmem((reps, arows, LANES), BF16),
        dma((7 + tps,)),
        dma((3, tps)),
        dma((tps,)),
        dma,
        dma,
        dma((steps, tps)),
        dma((steps, tps)),
        dma((3, tps)),
        dma((3, tps)),
        dma,
        dma,
        dma,
        dma,
        dma((2,)),
    ]
    operands = [
        hidden_in,
        key_cache.reshape(rows, capacity, head),
        value_cache.reshape(rows, capacity, head),
        query_weight,
        key_weight,
        value_weight,
        output_weight,
        norm_gain,
        countdown_table,
        countdown_ids,
        lengths,
        source_slot,
    ]
    return pl.pallas_call(
        functools.partial(kernel, reps, tps),
        out_shape=jax.ShapeDtypeStruct((steps, rows, model), BF16),
        in_specs=[pl.BlockSpec(memory_space=pl.ANY)] * 12,
        out_specs=pl.BlockSpec(memory_space=pl.ANY),
        scratch_shapes=scratch,
        compiler_params=pltpu.CompilerParams(
            collective_id=0, has_side_effects=True, vmem_limit_bytes=48 * 2**20
        ),
    )(
        *[pltpu.with_memory_space_constraint(x, pltpu.HBM) for x in operands]
    )


def solution(mesh):
    placed = (
        P("rep", None),
        P("rep", "tp", None, None),
        P("rep", "tp", None, None),
        P(None, "tp"),
        P(None, "tp"),
        P(None, "tp"),
        P("tp", None),
        P(),
        P(),
        P(None, "rep"),
        P(),
        P(),
    )
    return jax.shard_map(
        functools.partial(body, mesh.shape["rep"], mesh.shape["tp"]),
        mesh=mesh,
        in_specs=placed,
        out_specs=P(None, "rep", None),
        check_vma=False,
    )
```

```python
import functools
import math

import jax
import jax.numpy as jnp
from jax import lax
from jax.experimental import pallas as pl
from jax.experimental.pallas import tpu as pltpu
from jax.sharding import PartitionSpec as P

MESH = pl.DeviceIdType.MESH
F32 = jnp.float32
BF16 = jnp.bfloat16
THETA = 1000000.0
EPSILON = 1e-06
LANES = 128
MOVE = 2
KEEP = 4


def iota(shape, dim):
    return lax.broadcasted_iota(jnp.int32, shape, dim)


def ones_at(mask):
    return jnp.where(mask, 1.0, 0.0).astype(F32)


def lane_pick(index, row):
    lanes = iota((index.shape[0], row.shape[1]), 1)
    return jnp.sum(jnp.where(lanes == index, row, 0.0), axis=1, keepdims=True).astype(jnp.int32)


def pack(x):
    rows, width = x.shape
    high = (width // LANES + 1) // 2 * LANES
    low = jnp.concatenate([x[:, high:], jnp.zeros((rows, 2 * high - width), x.dtype)], axis=1)
    return jnp.concatenate([x[:, :high], low], axis=0).astype(BF16)


def unpack(y, width):
    y = y.astype(F32)
    rows, high = y.shape[0] // 2, y.shape[1]
    return jnp.concatenate([y[:rows], y[rows:, : width - high]], axis=1)


def stack_groups(x):
    return jnp.concatenate(
        [x[:, c : c + LANES] for c in range(0, x.shape[1], LANES)], axis=0
    )


def spread_groups(x, rows):
    return jnp.concatenate([x[c : c + rows] for c in range(0, x.shape[0], rows)], axis=1)


def dot(a, b):
    return jnp.dot(a, b, preferred_element_type=F32)


def kernel(
    reps,
    tps,
    hid_hbm,
    keys_hbm,
    values_hbm,
    wq_hbm,
    wk_hbm,
    wv_hbm,
    wo_hbm,
    gain_hbm,
    table_hbm,
    ids_hbm,
    len_hbm,
    src_hbm,
    out_hbm,
    hid_v,
    keys_v,
    values_v,
    wqkv_v,
    wo_v,
    gain_v,
    table_v,
    ids_v,
    len_s,
    src_v,
    gains_v,
    wide_v,
    sums_v,
    tab_v,
    rank_v,
    first_v,
    last_v,
    id_send,
    id_recv,
    part_send,
    part_recv,
    home_buf,
    first_buf,
    last_buf,
    row_send,
    row_recv,
    att_send,
    att_recv,
    load_sem,
    weight_sem,
    out_w_sem,
    id_ssem,
    id_rsem,
    part_ssem,
    part_rsem,
    gath_ssem,
    gath_rsem,
    row_ssem,
    row_rsem,
    att_ssem,
    att_rsem,
    out_sem,
):
    r = lax.axis_index("rep")
    t = lax.axis_index("tp")
    rows = hid_v.shape[0]
    chunk = wo_v.shape[2]
    groups = chunk // LANES
    heads = wo_v.shape[1] // LANES
    qcols = heads * LANES
    total_rows = rows * reps
    capacity = keys_v.shape[1]
    tokens = table_v.shape[1]
    model = chunk * tps
    half = LANES // 2
    erows = row_send.shape[0]
    arows = att_send.shape[0]

    def far_first(n):
        odd = lax.rem(n, 2)
        return tps // 2 + (lax.div(n, 2) + odd) * (1 - 2 * odd)

    sizes = (4, 4, 2) if reps == 32 else (reps,)

    def other_reps(visit):
        def partner(n):
            peer, stride = 0, 1
            for size in reversed(sizes):
                own = lax.rem(lax.div(r, stride), size)
                step = lax.rem(lax.div(n, stride), size) + size // 2
                peer = peer + lax.rem(own + step, size) * stride
                stride *= size
            return peer

        own, stride = 0, 1
        for size in reversed(sizes):
            own, stride = own + (size - size // 2) * stride, stride * size
        for low, high in ((0, own), (own + 1, reps)):

            @pl.loop(low, high)
            def _(n):
                visit(partner(n))

    barrier = pltpu.get_barrier_semaphore()

    def greet(to):
        pl.semaphore_signal(barrier, inc=1, device_id=to, device_id_type=MESH)

    other_reps(lambda peer: greet((peer, t)))

    @pl.loop(0, tps - 1)
    def _(n):
        greet((r, lax.rem(t + far_first(n), tps)))

    def chunk_cols(c):
        return pl.ds(pl.multiple_of(c * chunk, LANES), chunk)

    def chunk_rows(c):
        return pl.ds(pl.multiple_of(c * chunk, LANES), chunk)

    small = [
        pltpu.make_async_copy(src_hbm, src_v, load_sem.at[0]),
        pltpu.make_async_copy(ids_hbm, ids_v, load_sem.at[1]),
        pltpu.make_async_copy(len_hbm, len_s, load_sem.at[2]),
        pltpu.make_async_copy(hid_hbm, hid_v, load_sem.at[3]),
        pltpu.make_async_copy(gain_hbm, gain_v, load_sem.at[4]),
    ]
    for copy in small:
        copy.start()

    def table_copy(c):
        return pltpu.make_async_copy(
            table_hbm.at[:, chunk_cols(c)], table_v.at[c], load_sem.at[7 + c]
        )

    for c in range(tps):
        table_copy(c).start()

    def weight_copies(c):
        return [
            pltpu.make_async_copy(
                wq_hbm.at[chunk_rows(c), :], wqkv_v.at[c, :, pl.ds(0, qcols)], weight_sem.at[0, c]
            ),
            pltpu.make_async_copy(
                wk_hbm.at[chunk_rows(c), :], wqkv_v.at[c, :, pl.ds(qcols, LANES)], weight_sem.at[1, c]
            ),
            pltpu.make_async_copy(
                wv_hbm.at[chunk_rows(c), :],
                wqkv_v.at[c, :, pl.ds(qcols + LANES, LANES)],
                weight_sem.at[2, c],
            ),
        ]

    @pl.loop(0, tps)
    def _(c):
        for copy in weight_copies(c):
            copy.start()

    cache_copies = [
        pltpu.make_async_copy(keys_hbm, keys_v, load_sem.at[5]),
        pltpu.make_async_copy(values_hbm, values_v, load_sem.at[6]),
    ]
    for copy in cache_copies:
        copy.start()

    def out_weight_copy(c):
        return pltpu.make_async_copy(wo_hbm.at[:, chunk_cols(c)], wo_v.at[c], out_w_sem.at[c])

    @pl.loop(0, tps)
    def _(c):
        out_weight_copy(c).start()

    def to_all_reps(src, dst, send_sem, recv_sem):
        def send(peer):
            pltpu.make_async_remote_copy(
                src_ref=src,
                dst_ref=dst.at[r],
                send_sem=send_sem,
                recv_sem=recv_sem,
                device_id=(peer, t),
                device_id_type=MESH,
            ).start()

        other_reps(send)

    def wait_reps(dst, sem):
        blocks = dst.at[pl.ds(0, reps - 1)]
        pltpu.make_async_copy(blocks, blocks, sem).wait()

    small[0].wait()
    src0 = src_v[0:1, :].astype(F32)
    src1 = src_v[1:2, :].astype(F32)
    square = (total_rows, total_rows)
    subs, lanes = iota(square, 0), iota(square, 1)
    far = (subs >> 3) != (lanes >> 3)
    subs_f = subs.astype(F32)
    slot0 = ones_at(src0 == subs_f)
    slot1 = ones_at(src1 == subs_f)
    both = dot(slot0.astype(BF16), slot1.astype(BF16))
    leaves = jnp.where(far, slot0 + both, 0.0).astype(BF16)
    moved = ones_at(dot(leaves, jnp.ones((total_rows, LANES), BF16)) > 0.5)
    before = ones_at(((subs >> 3) == (lanes >> 3)) & (lanes < subs)).astype(BF16)
    rank = dot(before, moved.astype(BF16))
    rank_v[...] = jnp.where(moved > 0.5, rank, float(rows))

    row_of = iota((rows, total_rows), 0) + r * rows
    glanes = iota((rows, total_rows), 1)
    glanes_f = glanes.astype(F32)
    to0 = jnp.sum(jnp.where(src0 == row_of.astype(F32), glanes_f, 0.0), axis=1, keepdims=True)
    to1 = jnp.sum(jnp.where(src1 == to0, glanes_f, 0.0), axis=1, keepdims=True)
    to0, to1 = to0.astype(jnp.int32), to1.astype(jnp.int32)

    own_rank = rank_v[pl.ds(pl.multiple_of(r * rows, rows), rows), :]
    diagonal = iota((rows, LANES), 0) == (iota((rows, LANES), 1) & (rows - 1))
    rank_lane = jnp.sum(jnp.where(diagonal, own_rank, 0.0), axis=0, keepdims=True)

    def gather_sent(sent, kinds):
        shape = (sent, kinds * rows)
        p, q = iota(shape, 0), iota(shape, 1)
        want = (p & (KEEP - 1)).astype(F32)
        hit = ((p >> 2) == (q >> 3)) & (rank_lane[:, : kinds * rows] == want)
        return ones_at(hit).astype(BF16)

    row_pick = gather_sent(erows, groups)
    att_pick = gather_sent(arows, heads)

    def take_slots(kinds, sent, final):
        count = kinds * rows
        slot = r * rows + (iota((count, 1), 0) & (rows - 1))
        if final:
            slot = lane_pick(slot, src1)
        row = lane_pick(slot, src0)
        kind = iota((count, 1), 0) >> 3
        home = row >> 3
        one = ones_at(iota((count, total_rows), 1) == row).astype(BF16)
        k = dot(one, rank_v[...].astype(BF16)).astype(jnp.int32)[:, 0:1]
        far_at = jnp.where(home == r, -1, home * sent + kind * KEEP + k)
        near_at = jnp.where(home == r, kind * rows + (row & (rows - 1)), -1)
        from_far = ones_at(iota((count, reps * sent), 1) == far_at).astype(BF16)
        from_near = ones_at(iota((count, count), 1) == near_at).astype(BF16)
        return from_far, from_near

    first_far, first_near = take_slots(groups, erows, False)
    last_far, last_near = take_slots(groups, erows, True)
    att_far, att_near = take_slots(heads, arows, True)

    small[2].wait()
    sub8 = iota((rows, 1), 0)
    position = jnp.zeros((rows, 1), jnp.int32)
    for i in range(rows):
        position = jnp.where(sub8 == i, len_s[r * rows + i], position)
    lane128 = iota((1, LANES), 1)
    exponent = (lane128 & (half - 1)).astype(F32) * (-2.0 / LANES)
    frequency = jnp.exp(exponent * math.log(THETA))
    sign = jnp.where(lane128 < half, -1.0, 1.0)

    def turns(place):
        angles = place.astype(F32) * frequency
        return jnp.cos(angles), jnp.sin(angles) * sign

    small[1].wait()
    id_send[...] = jnp.zeros_like(id_send)
    id_send[:, 0:rows] = ids_v[...]
    pl.semaphore_wait(barrier, reps + tps - 2)

    to_all_reps(id_send, id_recv, id_ssem, id_rsem)
    id_recv[r] = id_send[...]

    token_lane = iota((rows, tokens), 1)

    def token_pick(ids):
        return ones_at(token_lane == ids)

    def hidden_chunk(c):
        return hid_v[:, chunk_cols(c)].astype(F32)

    lane8 = iota((rows, LANES), 1)

    def local_pick(step, slot):
        mine = jnp.where(lane8 == slot, id_send[step : step + 1, :].astype(F32), 0.0)
        return token_pick(jnp.sum(mine, axis=1, keepdims=True).astype(jnp.int32))

    stay_pick = local_pick(0, to0 & (rows - 1)).astype(BF16)
    slot_pick = local_pick(1, sub8)
    leaves0 = ones_at((to0 >> 3) != r)
    earlier = ones_at(iota((rows, rows), 1) < iota((rows, rows), 0)).astype(BF16)
    order = dot(earlier, jnp.broadcast_to(leaves0, (rows, LANES)).astype(BF16))[:, 0:1]
    movers = [(leaves0 > 0.5) & (order == float(k)) for k in range(MOVE)]
    for copy in small[3:]:
        copy.wait()
    gain = gain_v[...].astype(F32).reshape(1, model)
    for c in range(tps):
        table_copy(c).wait()
        gains_v[c] = jnp.broadcast_to(gain[:, c * chunk : (c + 1) * chunk], (rows, chunk))

    def gain_chunk(c):
        return gains_v[c, 0:1, :]

    def squares_of(mixture):
        sq = mixture * mixture
        return sum(sq[:, g * LANES : (g + 1) * LANES] for g in range(groups))

    def project(c, mixture, carry):
        acc, squares = carry
        scaled = (mixture * gain_chunk(c)).astype(BF16)
        return acc + dot(scaled, wqkv_v[c]), squares + squares_of(mixture)

    def normalise(carry):
        acc, squares = carry
        mean = jnp.sum(squares, axis=1, keepdims=True) * (1.0 / model)
        return acc * lax.rsqrt(mean + EPSILON)

    zero_carry = (jnp.zeros((rows, qcols + 2 * LANES), F32), jnp.zeros((rows, LANES), F32))
    scale = LANES**-0.5

    def round16(x):
        return x.astype(BF16).astype(F32)

    def attend(qkv, place, which, fresh):
        count = qkv.shape[0]
        cap_lane = iota((count, capacity), 1)
        cosine, sine = turns(place)

        def rotate(x):
            return round16(x * cosine + pltpu.roll(x, half, 1) * sine)

        queries = [rotate(qkv[:, h * LANES : (h + 1) * LANES]) for h in range(heads)]
        fresh_key = rotate(qkv[:, qcols : qcols + LANES])
        fresh_value = round16(qkv[:, qcols + LANES :])
        fresh = fresh + [(fresh_key, fresh_value, place)]
        stacked = jnp.concatenate(queries, axis=0).astype(BF16)
        scores = [jnp.zeros((count, capacity), F32)] * heads
        for i in range(rows):
            one = lax.dot_general(
                stacked, keys_v[i], (((1,), (1,)), ((), ())), preferred_element_type=F32
            )
            for h in range(heads):
                scores[h] = jnp.where(which == i, one[h * count : (h + 1) * count], scores[h])
        weights, extra, totals = [], [], []
        for h in range(heads):
            s = scores[h] * scale
            news = [jnp.sum(queries[h] * k, axis=1, keepdims=True) * scale for k, _, _ in fresh]
            for new, (_, _, at) in zip(news, fresh):
                s = jnp.where(cap_lane == at, new, s)
            s = jnp.where(cap_lane <= place, s, -jnp.inf)
            top = jnp.max(s, axis=1, keepdims=True)
            e = jnp.exp(s - top)
            totals.append(jnp.sum(e, axis=1, keepdims=True))
            for _, _, at in fresh:
                e = jnp.where(cap_lane == at, 0.0, e)
            weights.append(e)
            extra.append([round16(jnp.exp(new - top)) for new in news])
        stacked = jnp.concatenate(weights, axis=0).astype(BF16)
        outs = [jnp.zeros((count, LANES), F32)] * heads
        for i in range(rows):
            one = dot(stacked, values_v[i])
            for h in range(heads):
                outs[h] = jnp.where(which == i, one[h * count : (h + 1) * count], outs[h])
        for h in range(heads):
            for w, (_, v, _) in zip(extra[h], fresh):
                outs[h] = outs[h] + w * v
            outs[h] = round16(outs[h] / totals[h])
        return outs, fresh

    def part_copy(step, to, src):
        return pltpu.make_async_remote_copy(
            src_ref=part_send.at[step, to],
            dst_ref=part_recv.at[step, src],
            send_sem=part_ssem.at[step, to],
            recv_sem=part_rsem.at[step, src],
            device_id=(r, to),
            device_id_type=MESH,
        )

    def output_sum(step, attended, wait_weights, meanwhile):
        @pl.loop(0, tps - 1)
        def _(n):
            to = lax.rem(t + far_first(n), tps)
            if wait_weights:
                out_weight_copy(to).wait()
            part_send[step, to] = pack(dot(attended, wo_v[to]))
            part_copy(step, to, t).start()

        if wait_weights:
            out_weight_copy(t).wait()
        total = dot(attended, wo_v[t])
        meanwhile()

        def add(d, total):
            src = lax.rem(t + d, tps)
            part_copy(step, t, src).wait_recv()
            return total + unpack(part_recv[step, src], chunk)

        return lax.fori_loop(1, tps, add, total)

    def gather_copy(which, buf, to, src):
        return pltpu.make_async_remote_copy(
            src_ref=buf.at[src],
            dst_ref=buf.at[src],
            send_sem=gath_ssem.at[which, to],
            recv_sem=gath_rsem.at[which, src],
            device_id=(r, to),
            device_id_type=MESH,
        )

    def gather_start(which, buf, block):
        buf[t] = block

        @pl.loop(0, tps - 1)
        def _(n):
            gather_copy(which, buf, lax.rem(t + far_first(n), tps), t).start()

    sums_v[...] = jnp.zeros_like(sums_v)
    wide_v[...] = jnp.zeros_like(wide_v)

    @pl.loop(0, tps)
    def _(c):
        for copy in weight_copies(c):
            copy.wait()
        hid = hidden_chunk(c)
        table = table_v[c]
        blocks = [hid + dot(stay_pick, table)]
        for mover in movers:
            row = jnp.sum(jnp.where(mover, hid, 0.0), axis=0, keepdims=True)
            blocks.append(row + table.astype(F32))
        mixture = jnp.concatenate(blocks, axis=0)
        wide_v[...] += dot((mixture * gain_chunk(c)).astype(BF16), wqkv_v[c])
        sums_v[...] += squares_of(mixture)

    def mover_value(mover, column):
        return jnp.sum(jnp.where(mover, column, 0.0), axis=0, keepdims=True)

    def every_token(column):
        column = column.astype(F32)
        blocks = [column]
        for mover in movers:
            blocks.append(jnp.broadcast_to(mover_value(mover, column), (tokens, 1)))
        return jnp.concatenate(blocks, axis=0).astype(jnp.int32)

    wide = normalise((wide_v[...], sums_v[...]))
    for copy in cache_copies:
        copy.wait()
    outs, fresh = attend(wide, every_token(position), every_token(sub8), [])

    wait_reps(id_recv, id_rsem)

    def slot_tokens(step, slot):
        found = jnp.zeros((rows, LANES), F32)
        for h in range(reps):
            block = id_recv[h, step : step + 1, :].astype(F32)
            found = jnp.where((slot >> 3) == h, block, found)
        found = jnp.where(lane8 == (slot & (rows - 1)), found, 0.0)
        return jnp.sum(found, axis=1, keepdims=True)

    now = slot_tokens(0, to0)
    token_sub = iota((tokens, 1), 0).astype(F32)
    takes = [token_sub == mover_value(mover, now) for mover in movers]

    def choose(x):
        kept = x[0:rows]
        for k, (mover, take) in enumerate(zip(movers, takes)):
            block = x[rows + k * tokens : rows + (k + 1) * tokens]
            kept = jnp.where(mover, mover_value(take, block), kept)
        return kept

    attended = jnp.concatenate([choose(x) for x in outs], axis=1).astype(BF16)
    ((fresh_key, fresh_value, _),) = fresh
    fresh = [(choose(fresh_key), choose(fresh_value), position)]

    def find_tokens():
        next_pick = token_pick(slot_tokens(1, to1).astype(jnp.int32))
        picks = jnp.concatenate([next_pick, slot_pick], axis=0).astype(BF16)
        for c in range(tps):
            tab_v[c] = dot(picks, table_v[c])
        now_pick = token_pick(now.astype(jnp.int32)).astype(BF16)
        mix.append(hidden_chunk(t) + dot(now_pick, table_v[t]))

    mix = []
    summed = output_sum(0, attended, True, find_tokens)
    hidden = round16(mix[0] + summed)
    gather_start(0, home_buf, pack(hidden))
    own_groups = stack_groups(hidden).astype(BF16)
    row_send[...] = dot(row_pick, own_groups).astype(BF16)
    to_all_reps(row_send, row_recv, row_ssem, row_rsem)
    row_recv[r] = row_send[...]

    carry = project(t, hidden + tab_v[t, 0:rows], zero_carry)

    def next_project(n, carry):
        src = lax.rem(t + far_first(tps - 2 - n), tps)
        gather_copy(0, home_buf, t, src).wait_recv()
        return project(src, unpack(home_buf[src], chunk) + tab_v[src, 0:rows], carry)

    qkv = normalise(lax.fori_loop(0, tps - 1, next_project, carry))

    outs, _ = attend(qkv, position + 1, sub8, fresh)
    attended = jnp.concatenate(outs, axis=0).astype(BF16)
    att_send[...] = dot(att_pick, attended).astype(BF16)
    to_all_reps(att_send, att_recv, att_ssem, att_rsem)
    att_recv[r] = att_send[...]

    wait_reps(row_recv, row_rsem)
    received = row_recv[...].reshape(reps * erows, LANES)
    first = spread_groups(dot(first_far, received) + dot(first_near, own_groups), rows)
    last = spread_groups(dot(last_far, received) + dot(last_near, own_groups), rows)
    last = last + tab_v[t, rows:]
    gather_start(1, first_buf, pack(first))

    wait_reps(att_recv, att_rsem)
    received = att_recv[...].reshape(reps * arows, LANES)
    attended = (dot(att_far, received) + dot(att_near, attended)).astype(BF16)
    attended = spread_groups(attended, rows)

    def result(which, buf, out_v):
        @pl.loop(1, tps)
        def _(d):
            gather_copy(which, buf, t, lax.rem(t + d, tps)).wait_recv()

        for c in range(tps):
            cols = slice(c * chunk, (c + 1) * chunk)
            out_v[:, cols] = unpack(buf[c], chunk).astype(BF16)
        copy = pltpu.make_async_copy(out_v, out_hbm.at[which - 1], out_sem.at[which - 1])
        copy.start()
        return copy

    results = []
    summed = output_sum(1, attended, False, lambda: results.append(result(1, first_buf, first_v)))
    hidden = last + summed
    gather_start(2, last_buf, pack(hidden))
    results.append(result(2, last_buf, last_v))

    wait_reps(id_recv, id_ssem)
    wait_reps(row_recv, row_ssem)
    wait_reps(att_recv, att_ssem)

    @pl.loop(1, tps)
    def _(d):
        to = lax.rem(t + d, tps)
        for step in range(2):
            part_copy(step, to, t).wait_send()
        for which, buf in enumerate((home_buf, first_buf, last_buf)):
            gather_copy(which, buf, to, t).wait_send()

    for copy in results:
        copy.wait()


def body(
    reps,
    tps,
    hidden_in,
    key_cache,
    value_cache,
    query_weight,
    key_weight,
    value_weight,
    output_weight,
    norm_gain,
    countdown_table,
    countdown_ids,
    lengths,
    source_slot,
):
    rows, model = hidden_in.shape
    capacity, head = key_cache.shape[2:]
    chunk = model // tps
    qcols = query_weight.shape[1]
    heads = qcols // head
    tokens = countdown_table.shape[0]
    steps = countdown_ids.shape[0]
    total_rows = lengths.shape[0]
    groups = chunk // LANES
    high = (groups + 1) // 2 * LANES
    erows = -(-groups * KEEP // 16) * 16
    arows = -(-heads * KEEP // 16) * 16
    block = (2 * rows, high)
    dma, vmem = pltpu.SemaphoreType.DMA, pltpu.VMEM
    scratch = [
        vmem((rows, model), BF16),
        vmem((rows, capacity, head), BF16),
        vmem((rows, capacity, head), BF16),
        vmem((tps, chunk, qcols + 2 * head), BF16),
        vmem((tps, qcols, chunk), BF16),
        vmem((model,), BF16),
        vmem((tps, tokens, chunk), BF16),
        vmem((steps, rows), jnp.int32),
        pltpu.SMEM((total_rows,), jnp.int32),
        vmem((steps, total_rows), jnp.int32),
        vmem((tps, rows, chunk), F32),
        vmem((rows + MOVE * tokens, qcols + 2 * head), F32),
        vmem((rows + MOVE * tokens, LANES), F32),
        vmem((tps, 2 * rows, chunk), F32),
        vmem((total_rows, LANES), F32),
        vmem((rows, model), BF16),
        vmem((rows, model), BF16),
        vmem((steps, LANES), jnp.int32),
        vmem((reps, steps, LANES), jnp.int32),
        vmem((steps, tps) + block, BF16),
        vmem((steps, tps) + block, BF16),
        vmem((tps,) + block, BF16),
        vmem((tps,) + block, BF16),
        vmem((tps,) + block, BF16),
        vmem((erows, LANES), BF16),
        vmem((reps, erows, LANES), BF16),
        vmem((arows, LANES), BF16),
        vmem((reps, arows, LANES), BF16),
        dma((7 + tps,)),
        dma((3, tps)),
        dma((tps,)),
        dma,
        dma,
        dma((steps, tps)),
        dma((steps, tps)),
        dma((3, tps)),
        dma((3, tps)),
        dma,
        dma,
        dma,
        dma,
        dma((2,)),
    ]
    operands = [
        hidden_in,
        key_cache.reshape(rows, capacity, head),
        value_cache.reshape(rows, capacity, head),
        query_weight,
        key_weight,
        value_weight,
        output_weight,
        norm_gain,
        countdown_table,
        countdown_ids,
        lengths,
        source_slot,
    ]
    return pl.pallas_call(
        functools.partial(kernel, reps, tps),
        out_shape=jax.ShapeDtypeStruct((steps, rows, model), BF16),
        in_specs=[pl.BlockSpec(memory_space=pl.ANY)] * 12,
        out_specs=pl.BlockSpec(memory_space=pl.ANY),
        scratch_shapes=scratch,
        compiler_params=pltpu.CompilerParams(
            collective_id=0, has_side_effects=True, vmem_limit_bytes=48 * 2**20
        ),
    )(
        *[pltpu.with_memory_space_constraint(x, pltpu.HBM) for x in operands]
    )


def solution(mesh):
    placed = (
        P("rep", None),
        P("rep", "tp", None, None),
        P("rep", "tp", None, None),
        P(None, "tp"),
        P(None, "tp"),
        P(None, "tp"),
        P("tp", None),
        P(),
        P(),
        P(None, "rep"),
        P(),
        P(),
    )
    return jax.shard_map(
        functools.partial(body, mesh.shape["rep"], mesh.shape["tp"]),
        mesh=mesh,
        in_specs=placed,
        out_specs=P(None, "rep", None),
        check_vma=False,
    )
```

```python
import functools
import math

import jax
import jax.numpy as jnp
from jax import lax
from jax.experimental import pallas as pl
from jax.experimental.pallas import tpu as pltpu
from jax.sharding import PartitionSpec as P

MESH = pl.DeviceIdType.MESH
F32 = jnp.float32
BF16 = jnp.bfloat16
THETA = 1000000.0
EPSILON = 1e-06
LANES = 128
MOVE = 2
KEEP = 4


def iota(shape, dim):
    return lax.broadcasted_iota(jnp.int32, shape, dim)


def ones_at(mask):
    return jnp.where(mask, 1.0, 0.0).astype(F32)


def lane_pick(index, row):
    lanes = iota((index.shape[0], row.shape[1]), 1)
    return jnp.sum(jnp.where(lanes == index, row, 0.0), axis=1, keepdims=True).astype(jnp.int32)


def pack(x):
    rows, width = x.shape
    high = (width // LANES + 1) // 2 * LANES
    low = jnp.concatenate([x[:, high:], jnp.zeros((rows, 2 * high - width), x.dtype)], axis=1)
    return jnp.concatenate([x[:, :high], low], axis=0).astype(BF16)


def unpack(y, width):
    y = y.astype(F32)
    rows, high = y.shape[0] // 2, y.shape[1]
    return jnp.concatenate([y[:rows], y[rows:, : width - high]], axis=1)


def stack_groups(x):
    return jnp.concatenate(
        [x[:, c : c + LANES] for c in range(0, x.shape[1], LANES)], axis=0
    )


def spread_groups(x, rows):
    return jnp.concatenate([x[c : c + rows] for c in range(0, x.shape[0], rows)], axis=1)


def dot(a, b):
    return jnp.dot(a, b, preferred_element_type=F32)


def kernel(
    reps,
    tps,
    hid_hbm,
    keys_hbm,
    values_hbm,
    wq_hbm,
    wk_hbm,
    wv_hbm,
    wo_hbm,
    gain_hbm,
    table_hbm,
    ids_hbm,
    len_hbm,
    src_hbm,
    out_ref,
    hid_v,
    keys_v,
    values_v,
    wqkv_v,
    wo_v,
    gain_v,
    table_v,
    ids_v,
    len_s,
    src_v,
    gains_v,
    wide_v,
    sums_v,
    tab_v,
    rank_v,
    id_send,
    id_recv,
    part_send,
    part_recv,
    home_buf,
    first_buf,
    last_buf,
    row_send,
    row_recv,
    att_send,
    att_recv,
    load_sem,
    cache_sem,
    weight_sem,
    out_w_sem,
    id_ssem,
    id_rsem,
    part_ssem,
    part_rsem,
    gath_ssem,
    gath_rsem,
    row_ssem,
    row_rsem,
    att_ssem,
    att_rsem,
):
    r = lax.axis_index("rep")
    t = lax.axis_index("tp")
    rows = hid_v.shape[0]
    chunk = wo_v.shape[2]
    groups = chunk // LANES
    heads = wo_v.shape[1] // LANES
    qcols = heads * LANES
    total_rows = rows * reps
    capacity = keys_v.shape[1]
    tokens = table_v.shape[1]
    model = chunk * tps
    half = LANES // 2
    erows = row_send.shape[0]
    arows = att_send.shape[0]

    def far_first(n):
        odd = lax.rem(n, 2)
        return tps // 2 + (lax.div(n, 2) + odd) * (1 - 2 * odd)

    sizes = (4, 4, 2) if reps == 32 else (reps,)

    def other_reps(visit):
        def partner(n):
            peer, stride = 0, 1
            for size in reversed(sizes):
                own = lax.rem(lax.div(r, stride), size)
                step = lax.rem(lax.div(n, stride), size) + size // 2
                peer = peer + lax.rem(own + step, size) * stride
                stride *= size
            return peer

        own, stride = 0, 1
        for size in reversed(sizes):
            own, stride = own + (size - size // 2) * stride, stride * size
        for low, high in ((0, own), (own + 1, reps)):

            @pl.loop(low, high)
            def _(n):
                visit(partner(n))

    barrier = pltpu.get_barrier_semaphore()

    def greet(to):
        pl.semaphore_signal(barrier, inc=1, device_id=to, device_id_type=MESH)

    other_reps(lambda peer: greet((peer, t)))

    @pl.loop(0, tps - 1)
    def _(n):
        greet((r, lax.rem(t + far_first(n), tps)))

    def chunk_cols(c):
        return pl.ds(pl.multiple_of(c * chunk, LANES), chunk)

    def chunk_rows(c):
        return pl.ds(pl.multiple_of(c * chunk, LANES), chunk)

    small = [
        pltpu.make_async_copy(src_hbm, src_v, load_sem.at[0]),
        pltpu.make_async_copy(ids_hbm, ids_v, load_sem.at[1]),
        pltpu.make_async_copy(len_hbm, len_s, load_sem.at[2]),
        pltpu.make_async_copy(hid_hbm, hid_v, load_sem.at[3]),
        pltpu.make_async_copy(gain_hbm, gain_v, load_sem.at[4]),
    ]
    for copy in small:
        copy.start()

    def table_copy(c):
        return pltpu.make_async_copy(
            table_hbm.at[:, chunk_cols(c)], table_v.at[c], load_sem.at[7 + c]
        )

    for c in range(tps):
        table_copy(c).start()

    def weight_copies(c):
        return [
            pltpu.make_async_copy(
                wq_hbm.at[chunk_rows(c), :], wqkv_v.at[c, :, pl.ds(0, qcols)], weight_sem.at[0, c]
            ),
            pltpu.make_async_copy(
                wk_hbm.at[chunk_rows(c), :], wqkv_v.at[c, :, pl.ds(qcols, LANES)], weight_sem.at[1, c]
            ),
            pltpu.make_async_copy(
                wv_hbm.at[chunk_rows(c), :],
                wqkv_v.at[c, :, pl.ds(qcols + LANES, LANES)],
                weight_sem.at[2, c],
            ),
        ]

    @pl.loop(0, tps)
    def _(c):
        for copy in weight_copies(c):
            copy.start()

    cache_copies = [
        pltpu.make_async_copy(
            hbm.at[i], vmem.at[i // 2, :, pl.ds(i % 2 * LANES, LANES)], cache_sem.at[which, i]
        )
        for which, (hbm, vmem) in enumerate(((keys_hbm, keys_v), (values_hbm, values_v)))
        for i in range(rows)
    ]
    for copy in cache_copies:
        copy.start()

    def out_weight_copy(c):
        return pltpu.make_async_copy(wo_hbm.at[:, chunk_cols(c)], wo_v.at[c], out_w_sem.at[c])

    @pl.loop(0, tps)
    def _(c):
        out_weight_copy(c).start()

    def to_all_reps(src, dst, send_sem, recv_sem):
        def send(peer):
            pltpu.make_async_remote_copy(
                src_ref=src,
                dst_ref=dst.at[r],
                send_sem=send_sem,
                recv_sem=recv_sem,
                device_id=(peer, t),
                device_id_type=MESH,
            ).start()

        other_reps(send)

    def wait_reps(dst, sem):
        blocks = dst.at[pl.ds(0, reps - 1)]
        pltpu.make_async_copy(blocks, blocks, sem).wait()

    small[0].wait()
    src0 = src_v[0:1, :].astype(F32)
    src1 = src_v[1:2, :].astype(F32)
    square = (total_rows, total_rows)
    subs, lanes = iota(square, 0), iota(square, 1)
    far = (subs >> 3) != (lanes >> 3)
    subs_f = subs.astype(F32)
    slot0 = ones_at(src0 == subs_f)
    slot1 = ones_at(src1 == subs_f)
    both = dot(slot0.astype(BF16), slot1.astype(BF16))
    leaves = jnp.where(far, slot0 + both, 0.0).astype(BF16)
    moved = ones_at(dot(leaves, jnp.ones((total_rows, LANES), BF16)) > 0.5)
    before = ones_at(((subs >> 3) == (lanes >> 3)) & (lanes < subs)).astype(BF16)
    rank = dot(before, moved.astype(BF16))
    rank_v[...] = jnp.where(moved > 0.5, rank, float(rows))

    row_of = iota((rows, total_rows), 0) + r * rows
    glanes = iota((rows, total_rows), 1)
    glanes_f = glanes.astype(F32)
    to0 = jnp.sum(jnp.where(src0 == row_of.astype(F32), glanes_f, 0.0), axis=1, keepdims=True)
    to1 = jnp.sum(jnp.where(src1 == to0, glanes_f, 0.0), axis=1, keepdims=True)
    to0, to1 = to0.astype(jnp.int32), to1.astype(jnp.int32)

    own_rank = rank_v[pl.ds(pl.multiple_of(r * rows, rows), rows), :]
    diagonal = iota((rows, LANES), 0) == (iota((rows, LANES), 1) & (rows - 1))
    rank_lane = jnp.sum(jnp.where(diagonal, own_rank, 0.0), axis=0, keepdims=True)

    def gather_sent(sent, kinds):
        shape = (sent, kinds * rows)
        p, q = iota(shape, 0), iota(shape, 1)
        want = (p & (KEEP - 1)).astype(F32)
        hit = ((p >> 2) == (q >> 3)) & (rank_lane[:, : kinds * rows] == want)
        return ones_at(hit).astype(BF16)

    row_pick = gather_sent(erows, groups)
    att_pick = gather_sent(arows, heads)

    def take_slots(kinds, sent, final):
        count = kinds * rows
        slot = r * rows + (iota((count, 1), 0) & (rows - 1))
        if final:
            slot = lane_pick(slot, src1)
        row = lane_pick(slot, src0)
        kind = iota((count, 1), 0) >> 3
        home = row >> 3
        one = ones_at(iota((count, total_rows), 1) == row).astype(BF16)
        k = dot(one, rank_v[...].astype(BF16)).astype(jnp.int32)[:, 0:1]
        far_at = jnp.where(home == r, -1, home * sent + kind * KEEP + k)
        near_at = jnp.where(home == r, kind * rows + (row & (rows - 1)), -1)
        from_far = ones_at(iota((count, reps * sent), 1) == far_at).astype(BF16)
        from_near = ones_at(iota((count, count), 1) == near_at).astype(BF16)
        return from_far, from_near

    first_far, first_near = take_slots(groups, erows, False)
    last_far, last_near = take_slots(groups, erows, True)
    att_far, att_near = take_slots(heads, arows, True)

    small[2].wait()
    sub8 = iota((rows, 1), 0)
    position = jnp.zeros((rows, 1), jnp.int32)
    for i in range(rows):
        position = jnp.where(sub8 == i, len_s[r * rows + i], position)
    lane128 = iota((1, LANES), 1)
    exponent = (lane128 & (half - 1)).astype(F32) * (-2.0 / LANES)
    frequency = jnp.exp(exponent * math.log(THETA))
    sign = jnp.where(lane128 < half, -1.0, 1.0)

    def turns(place):
        angles = place.astype(F32) * frequency
        return jnp.cos(angles), jnp.sin(angles) * sign

    small[1].wait()
    id_send[...] = jnp.zeros_like(id_send)
    id_send[:, 0:rows] = ids_v[...]
    pl.semaphore_wait(barrier, reps + tps - 2)

    to_all_reps(id_send, id_recv, id_ssem, id_rsem)
    id_recv[r] = id_send[...]

    token_lane = iota((rows, tokens), 1)

    def token_pick(ids):
        return ones_at(token_lane == ids)

    def hidden_chunk(c):
        return hid_v[:, chunk_cols(c)].astype(F32)

    lane8 = iota((rows, LANES), 1)

    def local_pick(step, slot):
        mine = jnp.where(lane8 == slot, id_send[step : step + 1, :].astype(F32), 0.0)
        return token_pick(jnp.sum(mine, axis=1, keepdims=True).astype(jnp.int32))

    stay_pick = local_pick(0, to0 & (rows - 1)).astype(BF16)
    slot_pick = local_pick(1, sub8)
    leaves0 = ones_at((to0 >> 3) != r)
    earlier = ones_at(iota((rows, rows), 1) < iota((rows, rows), 0)).astype(BF16)
    order = dot(earlier, jnp.broadcast_to(leaves0, (rows, LANES)).astype(BF16))[:, 0:1]
    movers = [(leaves0 > 0.5) & (order == float(k)) for k in range(MOVE)]
    for copy in small[3:]:
        copy.wait()
    gain = gain_v[...].astype(F32).reshape(1, model)
    for c in range(tps):
        table_copy(c).wait()
        gains_v[c] = jnp.broadcast_to(gain[:, c * chunk : (c + 1) * chunk], (rows, chunk))

    def gain_chunk(c):
        return gains_v[c, 0:1, :]

    def squares_of(mixture):
        sq = mixture * mixture
        return sum(sq[:, g * LANES : (g + 1) * LANES] for g in range(groups))

    def project(c, mixture, carry):
        acc, squares = carry
        scaled = (mixture * gain_chunk(c)).astype(BF16)
        return acc + dot(scaled, wqkv_v[c]), squares + squares_of(mixture)

    def normalise(carry):
        acc, squares = carry
        mean = jnp.sum(squares, axis=1, keepdims=True) * (1.0 / model)
        return acc * lax.rsqrt(mean + EPSILON)

    zero_carry = (jnp.zeros((rows, qcols + 2 * LANES), F32), jnp.zeros((rows, LANES), F32))
    scale = LANES**-0.5

    def round16(x):
        return x.astype(BF16).astype(F32)

    def attend(qkv, place, which, fresh):
        count = qkv.shape[0]
        cap_lane = iota((count, capacity), 1)
        cosine, sine = turns(place)

        def rotate(x):
            return round16(x * cosine + pltpu.roll(x, half, 1) * sine)

        queries = [rotate(qkv[:, h * LANES : (h + 1) * LANES]) for h in range(heads)]
        fresh_key = rotate(qkv[:, qcols : qcols + LANES])
        fresh_value = round16(qkv[:, qcols + LANES :])
        fresh = fresh + [(fresh_key, fresh_value, place)]
        stacked = jnp.concatenate(queries, axis=0).astype(BF16)
        scores = [jnp.zeros((count, capacity), F32)] * heads
        none = jnp.zeros_like(stacked)
        sides = jnp.concatenate(
            [
                jnp.concatenate([stacked, none], axis=1),
                jnp.concatenate([none, stacked], axis=1),
            ],
            axis=0,
        )
        for pair in range(rows // 2):
            both = lax.dot_general(
                sides, keys_v[pair], (((1,), (1,)), ((), ())), preferred_element_type=F32
            )
            for side in range(2):
                for h in range(heads):
                    at = (side * heads + h) * count
                    scores[h] = jnp.where(
                        which == 2 * pair + side, both[at : at + count], scores[h]
                    )
        weights, extra, totals = [], [], []
        for h in range(heads):
            s = scores[h] * scale
            news = [jnp.sum(queries[h] * k, axis=1, keepdims=True) * scale for k, _, _ in fresh]
            for new, (_, _, at) in zip(news, fresh):
                s = jnp.where(cap_lane == at, new, s)
            s = jnp.where(cap_lane <= place, s, -jnp.inf)
            top = jnp.max(s, axis=1, keepdims=True)
            e = jnp.exp(s - top)
            totals.append(jnp.sum(e, axis=1, keepdims=True))
            for _, _, at in fresh:
                e = jnp.where(cap_lane == at, 0.0, e)
            weights.append(e)
            extra.append([round16(jnp.exp(new - top)) for new in news])
        stacked = jnp.concatenate(weights, axis=0).astype(BF16)
        outs = [jnp.zeros((count, LANES), F32)] * heads
        for pair in range(rows // 2):
            both = dot(stacked, values_v[pair])
            for side in range(2):
                one = both[:, side * LANES : (side + 1) * LANES]
                for h in range(heads):
                    outs[h] = jnp.where(
                        which == 2 * pair + side, one[h * count : (h + 1) * count], outs[h]
                    )
        for h in range(heads):
            for w, (_, v, _) in zip(extra[h], fresh):
                outs[h] = outs[h] + w * v
            outs[h] = round16(outs[h] / totals[h])
        return outs, fresh

    def part_copy(step, to, src):
        return pltpu.make_async_remote_copy(
            src_ref=part_send.at[step, to],
            dst_ref=part_recv.at[step, src],
            send_sem=part_ssem.at[step, to],
            recv_sem=part_rsem.at[step, src],
            device_id=(r, to),
            device_id_type=MESH,
        )

    def output_sum(step, attended, wait_weights, meanwhile):
        @pl.loop(0, tps - 1)
        def _(n):
            to = lax.rem(t + far_first(n), tps)
            if wait_weights:
                out_weight_copy(to).wait()
            part_send[step, to] = pack(dot(attended, wo_v[to]))
            part_copy(step, to, t).start()

        if wait_weights:
            out_weight_copy(t).wait()
        total = dot(attended, wo_v[t])
        meanwhile()

        def add(d, total):
            src = lax.rem(t + d, tps)
            part_copy(step, t, src).wait_recv()
            return total + unpack(part_recv[step, src], chunk)

        return lax.fori_loop(1, tps, add, total)

    def gather_copy(which, buf, to, src):
        return pltpu.make_async_remote_copy(
            src_ref=buf.at[src],
            dst_ref=buf.at[src],
            send_sem=gath_ssem.at[which, to],
            recv_sem=gath_rsem.at[which, src],
            device_id=(r, to),
            device_id_type=MESH,
        )

    def gather_start(which, buf, block):
        buf[t] = block

        @pl.loop(0, tps - 1)
        def _(n):
            gather_copy(which, buf, lax.rem(t + far_first(n), tps), t).start()

    sums_v[...] = jnp.zeros_like(sums_v)
    wide_v[...] = jnp.zeros_like(wide_v)

    @pl.loop(0, tps)
    def _(c):
        for copy in weight_copies(c):
            copy.wait()
        hid = hidden_chunk(c)
        table = table_v[c]
        blocks = [hid + dot(stay_pick, table)]
        for mover in movers:
            row = jnp.sum(jnp.where(mover, hid, 0.0), axis=0, keepdims=True)
            blocks.append(row + table.astype(F32))
        mixture = jnp.concatenate(blocks, axis=0)
        wide_v[...] += dot((mixture * gain_chunk(c)).astype(BF16), wqkv_v[c])
        sums_v[...] += squares_of(mixture)

    def mover_value(mover, column):
        return jnp.sum(jnp.where(mover, column, 0.0), axis=0, keepdims=True)

    def every_token(column):
        column = column.astype(F32)
        blocks = [column]
        for mover in movers:
            blocks.append(jnp.broadcast_to(mover_value(mover, column), (tokens, 1)))
        return jnp.concatenate(blocks, axis=0).astype(jnp.int32)

    wide = normalise((wide_v[...], sums_v[...]))
    for copy in cache_copies:
        copy.wait()
    outs, fresh = attend(wide, every_token(position), every_token(sub8), [])

    wait_reps(id_recv, id_rsem)

    def slot_tokens(step, slot):
        found = jnp.zeros((rows, LANES), F32)
        for h in range(reps):
            block = id_recv[h, step : step + 1, :].astype(F32)
            found = jnp.where((slot >> 3) == h, block, found)
        found = jnp.where(lane8 == (slot & (rows - 1)), found, 0.0)
        return jnp.sum(found, axis=1, keepdims=True)

    now = slot_tokens(0, to0)
    token_sub = iota((tokens, 1), 0).astype(F32)
    takes = [token_sub == mover_value(mover, now) for mover in movers]

    def choose(x):
        kept = x[0:rows]
        for k, (mover, take) in enumerate(zip(movers, takes)):
            block = x[rows + k * tokens : rows + (k + 1) * tokens]
            kept = jnp.where(mover, mover_value(take, block), kept)
        return kept

    attended = jnp.concatenate([choose(x) for x in outs], axis=1).astype(BF16)
    ((fresh_key, fresh_value, _),) = fresh
    fresh = [(choose(fresh_key), choose(fresh_value), position)]

    def find_tokens():
        next_pick = token_pick(slot_tokens(1, to1).astype(jnp.int32))
        picks = jnp.concatenate([next_pick, slot_pick], axis=0).astype(BF16)
        for c in range(tps):
            tab_v[c] = dot(picks, table_v[c])
        now_pick = token_pick(now.astype(jnp.int32)).astype(BF16)
        mix.append(hidden_chunk(t) + dot(now_pick, table_v[t]))

    mix = []
    summed = output_sum(0, attended, True, find_tokens)
    hidden = round16(mix[0] + summed)
    gather_start(0, home_buf, pack(hidden))
    own_groups = stack_groups(hidden).astype(BF16)
    row_send[...] = dot(row_pick, own_groups).astype(BF16)
    to_all_reps(row_send, row_recv, row_ssem, row_rsem)
    row_recv[r] = row_send[...]

    carry = project(t, hidden + tab_v[t, 0:rows], zero_carry)

    def next_project(n, carry):
        src = lax.rem(t + far_first(tps - 2 - n), tps)
        gather_copy(0, home_buf, t, src).wait_recv()
        return project(src, unpack(home_buf[src], chunk) + tab_v[src, 0:rows], carry)

    qkv = normalise(lax.fori_loop(0, tps - 1, next_project, carry))

    outs, _ = attend(qkv, position + 1, sub8, fresh)
    attended = jnp.concatenate(outs, axis=0).astype(BF16)
    att_send[...] = dot(att_pick, attended).astype(BF16)
    to_all_reps(att_send, att_recv, att_ssem, att_rsem)
    att_recv[r] = att_send[...]

    wait_reps(row_recv, row_rsem)
    received = row_recv[...].reshape(reps * erows, LANES)
    first = spread_groups(dot(first_far, received) + dot(first_near, own_groups), rows)
    last = spread_groups(dot(last_far, received) + dot(last_near, own_groups), rows)
    last = last + tab_v[t, rows:]
    gather_start(1, first_buf, pack(first))

    wait_reps(att_recv, att_rsem)
    received = att_recv[...].reshape(reps * arows, LANES)
    attended = (dot(att_far, received) + dot(att_near, attended)).astype(BF16)
    attended = spread_groups(attended, rows)

    def result(which, buf):
        @pl.loop(1, tps)
        def _(d):
            gather_copy(which, buf, t, lax.rem(t + d, tps)).wait_recv()

        for c in range(tps):
            cols = slice(c * chunk, (c + 1) * chunk)
            out_ref[which - 1, :, cols] = unpack(buf[c], chunk).astype(BF16)

    summed = output_sum(1, attended, False, lambda: result(1, first_buf))
    hidden = last + summed
    gather_start(2, last_buf, pack(hidden))
    result(2, last_buf)

    wait_reps(id_recv, id_ssem)
    wait_reps(row_recv, row_ssem)
    wait_reps(att_recv, att_ssem)

    @pl.loop(1, tps)
    def _(d):
        to = lax.rem(t + d, tps)
        for step in range(2):
            part_copy(step, to, t).wait_send()
        for which, buf in enumerate((home_buf, first_buf, last_buf)):
            gather_copy(which, buf, to, t).wait_send()


def body(
    reps,
    tps,
    hidden_in,
    key_cache,
    value_cache,
    query_weight,
    key_weight,
    value_weight,
    output_weight,
    norm_gain,
    countdown_table,
    countdown_ids,
    lengths,
    source_slot,
):
    rows, model = hidden_in.shape
    capacity, head = key_cache.shape[2:]
    chunk = model // tps
    qcols = query_weight.shape[1]
    heads = qcols // head
    tokens = countdown_table.shape[0]
    steps = countdown_ids.shape[0]
    total_rows = lengths.shape[0]
    groups = chunk // LANES
    high = (groups + 1) // 2 * LANES
    erows = -(-groups * KEEP // 16) * 16
    arows = -(-heads * KEEP // 16) * 16
    block = (2 * rows, high)
    dma, vmem = pltpu.SemaphoreType.DMA, pltpu.VMEM
    scratch = [
        vmem((rows, model), BF16),
        vmem((rows // 2, capacity, 2 * head), BF16),
        vmem((rows // 2, capacity, 2 * head), BF16),
        vmem((tps, chunk, qcols + 2 * head), BF16),
        vmem((tps, qcols, chunk), BF16),
        vmem((model,), BF16),
        vmem((tps, tokens, chunk), BF16),
        vmem((steps, rows), jnp.int32),
        pltpu.SMEM((total_rows,), jnp.int32),
        vmem((steps, total_rows), jnp.int32),
        vmem((tps, rows, chunk), F32),
        vmem((rows + MOVE * tokens, qcols + 2 * head), F32),
        vmem((rows + MOVE * tokens, LANES), F32),
        vmem((tps, 2 * rows, chunk), F32),
        vmem((total_rows, LANES), F32),
        vmem((steps, LANES), jnp.int32),
        vmem((reps, steps, LANES), jnp.int32),
        vmem((steps, tps) + block, BF16),
        vmem((steps, tps) + block, BF16),
        vmem((tps,) + block, BF16),
        vmem((tps,) + block, BF16),
        vmem((tps,) + block, BF16),
        vmem((erows, LANES), BF16),
        vmem((reps, erows, LANES), BF16),
        vmem((arows, LANES), BF16),
        vmem((reps, arows, LANES), BF16),
        dma((7 + tps,)),
        dma((2, rows)),
        dma((3, tps)),
        dma((tps,)),
        dma,
        dma,
        dma((steps, tps)),
        dma((steps, tps)),
        dma((3, tps)),
        dma((3, tps)),
        dma,
        dma,
        dma,
        dma,
    ]
    operands = [
        hidden_in,
        key_cache.reshape(rows, capacity, head),
        value_cache.reshape(rows, capacity, head),
        query_weight,
        key_weight,
        value_weight,
        output_weight,
        norm_gain,
        countdown_table,
        countdown_ids,
        lengths,
        source_slot,
    ]
    return pl.pallas_call(
        functools.partial(kernel, reps, tps),
        out_shape=pltpu.VMEM((steps, rows, model), BF16),
        in_specs=[pl.BlockSpec(memory_space=pl.ANY)] * 12,
        out_specs=pl.BlockSpec(memory_space=pltpu.VMEM),
        scratch_shapes=scratch,
        compiler_params=pltpu.CompilerParams(
            collective_id=0, has_side_effects=True, vmem_limit_bytes=48 * 2**20
        ),
    )(
        *[pltpu.with_memory_space_constraint(x, pltpu.HBM) for x in operands]
    )


def solution(mesh):
    placed = (
        P("rep", None),
        P("rep", "tp", None, None),
        P("rep", "tp", None, None),
        P(None, "tp"),
        P(None, "tp"),
        P(None, "tp"),
        P("tp", None),
        P(),
        P(),
        P(None, "rep"),
        P(),
        P(),
    )
    return jax.shard_map(
        functools.partial(body, mesh.shape["rep"], mesh.shape["tp"]),
        mesh=mesh,
        in_specs=placed,
        out_specs=P(None, "rep", None),
        check_vma=False,
    )
```
